256 devices in a mesh: group: 16 (over z, core), dev: 16 (over y, x).
Axes of the slice: x: 4, y: 4, z: 8, core: 2. Of those that a mesh axis runs over, the one named last changes fastest.
Arguments:
- applied_loads: float32 [256, 1536, 128], P(('group', 'dev'))
- stiffness: bfloat16 [256, 1536, 1536], P(('group', 'dev')), as said below
- local_inverse: bfloat16 [256, 1536, 1536], P(('group', 'dev')), as said below
- coarse_basis: bfloat16 [256, 48, 1536], P(('group', 'dev')), may hold values from -0.15625 to 0.15625
- face_index: int32 [256, 1536], P(('group', 'dev')), may hold values from 0 to 1535, each once within a row
- coarse_map: int32 [256, 48], P(('group', 'dev')), may hold values from 0 to 47, each once within a row
- group_inverse: float32 [12288, 768], P(('group', 'dev')), as said below
- top_basis: float32 [12288, 48], P(('group', 'dev')), may hold values from -0.875 to 0.875
- top_inverse: float32 [768, 768], P('group'), as said below
Outputs:
- solution: float32 [256, 1536, 128], P(('group', 'dev'))
- residual: float32 [256, 1536, 128], P(('group', 'dev'))
- direction: float32 [256, 1536, 128], P(('group', 'dev'))
The draws below stay inside these ranges and needn't reach their ends.
Inputs may be any that keep to these rules, and one draw needn't show every extreme that they name: `stiffness`: each subdomain's block is symmetric positive definite. `local_inverse`: each subdomain's block is symmetric positive definite. `group_inverse`: each group's block of 768 rows is symmetric positive definite. `top_inverse`: symmetric positive definite. `face_index`: each row is a permutation. `coarse_map`: each row is a permutation.
All inputs are finite; a program needn't handle non-finite values.
Results may differ from the reference program's by a relative error of at most 0.0081.
The reference program's roundings to bfloat16 on the way count: a program that leaves them out, or rounds other values in their place, can miss the bound.
Values sent between devices are 32-bit elements; how exact they have to be, the bound alone decides.
A program may use at most 64 MiB of HBM per device.

```python
import math
import jax
import jax.numpy as jnp
from jax import lax

NI = 1536
NCON = 48
TOPC = 48
NRHS = 128
ITERS = 2
FACE = 384
SUBS = 256
GC = 768
TOPN = 768
N_GROUP = 16
N_DEV = 16


def spd_block(key, order, lowest, highest, spread):
    diag_key, noise_key = jax.random.split(key)
    diagonal = jax.random.uniform(diag_key, (order,), jnp.float32, lowest, highest)
    noise = jax.random.truncated_normal(noise_key, -4.0, 4.0, (order, order), jnp.float32)
    symmetric = (noise + noise.T) * (spread / math.sqrt(2.0 * order))
    return symmetric + jnp.diag(diagonal)


def spd_stack(key, count, order, lowest, highest, spread, out_type):
    block_keys = jax.random.split(key, count)
    return lax.map(lambda one_key: spd_block(one_key, order, lowest, highest, spread).astype(out_type), block_keys)


def draw_applied_loads(key, part):
    key = jax.random.fold_in(key, 11)
    base_key, hot_key = jax.random.split(key)
    placing = jnp.arange(SUBS, dtype=jnp.float32) / max(SUBS - 1, 1)
    rising = 3.0 ** (placing - 0.5)
    hottest = jax.random.randint(hot_key, (NRHS,), 0, SUBS)
    boost = jnp.where(jnp.arange(SUBS)[:, None] == hottest[None, :], 3.0, 1.0)
    scaling = rising[:, None] * boost
    base = jax.random.normal(base_key, (SUBS, NI, NRHS), jnp.float32)
    return (base * scaling[:, None, :]).astype(jnp.float32)


def draw_stiffness(key, part):
    key = jax.random.fold_in(key, 3)
    return spd_stack(key, SUBS, NI, 1.0, 2.5, 0.4, jnp.bfloat16)


def draw_local_inverse(key, part):
    key = jax.random.fold_in(key, 5)
    return spd_stack(key, SUBS, NI, 0.4, 1.0, 0.16, jnp.bfloat16)


def draw_group_inverse(key, part):
    key = jax.random.fold_in(key, 7)
    stacked = spd_stack(key, N_GROUP, GC, 0.4, 1.0, 0.16, jnp.float32)
    return stacked.reshape(N_GROUP * GC, GC)


def draw_top_inverse(key, part):
    key = jax.random.fold_in(key, 9)
    return spd_block(key, TOPN, 0.4, 1.0, 0.16).astype(jnp.float32)


def shard_levels(key, dims, pieces, smallest, top_value):
    loudness, own = 1.0, jax.random.fold_in(key, 6)
    for axis_at, blocks in pieces:
        heights = jnp.exp(jax.random.uniform(jax.random.fold_in(own, axis_at), (blocks,), jnp.float32, smallest / len(pieces), top_value / len(pieces)))
        loudness = loudness * jnp.repeat(heights, dims[axis_at] // blocks).reshape([-1 if axis == axis_at else 1 for axis in range(len(dims))])
    return loudness


def normal_values(stream_key, extent, deviation, limit, cuts=(), held_as=jnp.bfloat16):
    values = deviation * jax.random.normal(stream_key, extent, jnp.float32)
    if cuts:
        values = values * shard_levels(stream_key, extent, cuts, -0.22, 0.18)
    return jnp.clip(values, -limit, limit).astype(held_as)


def setup_inputs(seed: int = 0) -> dict:
    streams_of = jax.random.split(jax.random.key(seed), 10)
    applied_loads = draw_applied_loads(jax.random.fold_in(streams_of[9], 71), 0)
    stiffness = draw_stiffness(jax.random.fold_in(streams_of[9], 71), 0)
    local_inverse = draw_local_inverse(jax.random.fold_in(streams_of[9], 71), 0)
    coarse_basis = normal_values(streams_of[3], (SUBS, NCON, NI), NI ** -0.5, 0.15625, ((0, 256),))
    face_index = jax.vmap(lambda own: jax.random.permutation(own, NI))(jax.random.split(streams_of[4], SUBS)).reshape((SUBS, NI)).astype(jnp.int32)
    coarse_map = jax.vmap(lambda own: jax.random.permutation(own, NCON))(jax.random.split(streams_of[5], SUBS)).reshape((SUBS, NCON)).astype(jnp.int32)
    group_inverse = draw_group_inverse(jax.random.fold_in(streams_of[9], 71), 0)
    top_basis = normal_values(streams_of[7], (N_GROUP * GC, TOPC), TOPC ** -0.5, 0.875, ((0, 256),), jnp.float32)
    top_inverse = draw_top_inverse(jax.random.fold_in(streams_of[9], 71), 0)
    return {"applied_loads": applied_loads, "stiffness": stiffness, "local_inverse": local_inverse, "coarse_basis": coarse_basis, "face_index": face_index, "coarse_map": coarse_map, "group_inverse": group_inverse, "top_basis": top_basis, "top_inverse": top_inverse}


HIGHEST_PRECISION = lax.Precision.HIGHEST


def shift_lower(field, axis_number):
    zero_slab = jnp.zeros_like(lax.slice_in_dim(field, 0, 1, axis=axis_number))
    remainder = lax.slice_in_dim(field, 0, field.shape[axis_number] - 1, axis=axis_number)
    return jnp.concatenate([zero_slab, remainder], axis=axis_number)


def shift_higher(field, axis_number):
    zero_slab = jnp.zeros_like(lax.slice_in_dim(field, 0, 1, axis=axis_number))
    remainder = lax.slice_in_dim(field, 1, field.shape[axis_number], axis=axis_number)
    return jnp.concatenate([remainder, zero_slab], axis=axis_number)


def assemble(field, face_index):
    ordered = jnp.take_along_axis(field, face_index[:, :, None], axis=1)
    ordered = ordered.reshape(N_GROUP, N_DEV, 4, FACE, NRHS)
    partner = jnp.stack([shift_lower(ordered[:, :, 1], 1), shift_higher(ordered[:, :, 0], 1),
                         shift_lower(ordered[:, :, 3], 0), shift_higher(ordered[:, :, 2], 0)], axis=2)
    partner = partner.reshape(SUBS, NI, NRHS)
    return jax.vmap(lambda target, places, addend: target.at[places].add(addend))(field, face_index, partner)


def multiplicity(face_index):
    group_of = jnp.arange(SUBS, dtype=jnp.int32) // N_DEV
    dev_of = jnp.arange(SUBS, dtype=jnp.int32) % N_DEV
    neighbours = jnp.stack([dev_of > 0, dev_of < N_DEV - 1, group_of > 0, group_of < N_GROUP - 1], axis=1)
    face_weight = jnp.repeat(jnp.where(neighbours, 0.5, 1.0).astype(jnp.float32), FACE, axis=1)
    return jax.vmap(lambda places, entries: jnp.zeros((NI,), jnp.float32).at[places].set(entries))(face_index, face_weight)


def inner_product(left_side, right_side, weights):
    return jnp.sum(weights[:, :, None] * left_side * right_side, axis=(0, 1))


def precondition(residual, weights, local_inverse, coarse_basis, face_index, coarse_map, group_inverse, top_basis, top_inverse):
    scaled_res = (weights[:, :, None] * residual).astype(jnp.bfloat16)
    coarse_part = jnp.einsum("sci,sin->scn", coarse_basis.astype(jnp.float32), scaled_res.astype(jnp.float32), precision=HIGHEST_PRECISION)
    selector = (coarse_map[:, :, None] == jnp.arange(NCON, dtype=jnp.int32)[None, None, :]).astype(jnp.float32)
    ordered = jnp.einsum("sjk,sjn->skn", selector, coarse_part, precision=HIGHEST_PRECISION).reshape(N_GROUP, GC, NRHS)
    group_mats = group_inverse.reshape(N_GROUP, GC, GC)
    solved = jnp.einsum("gab,gbn->gan", group_mats, ordered, precision=HIGHEST_PRECISION)
    top_mats = top_basis.reshape(N_GROUP, GC, TOPC)
    reduced = jnp.einsum("gat,gan->gtn", top_mats, ordered, precision=HIGHEST_PRECISION).reshape(TOPN, NRHS)
    upper = jnp.dot(top_inverse, reduced, precision=HIGHEST_PRECISION).reshape(N_GROUP, TOPC, NRHS)
    corrected = solved + jnp.einsum("gat,gtn->gan", top_mats, upper, precision=HIGHEST_PRECISION)
    own_values = jnp.einsum("sjk,skn->sjn", selector, corrected.reshape(SUBS, NCON, NRHS), precision=HIGHEST_PRECISION)

    def one_subdomain(items):
        inverse_block, scaled_block, basis_block, value_block = items
        local_part = jnp.dot(inverse_block, scaled_block, preferred_element_type=jnp.float32)
        return local_part + jnp.dot(basis_block.astype(jnp.float32).T, value_block, precision=HIGHEST_PRECISION)

    combined = lax.map(one_subdomain, (local_inverse, scaled_res, coarse_basis, own_values))
    return assemble(weights[:, :, None] * combined, face_index)


def reference(applied_loads, stiffness, local_inverse, coarse_basis, face_index, coarse_map, group_inverse, top_basis, top_inverse):
    weights = multiplicity(face_index)

    def apply_precond(field):
        return precondition(field, weights, local_inverse, coarse_basis, face_index, coarse_map, group_inverse, top_basis, top_inverse)

    residual = assemble(applied_loads, face_index)
    solution = jnp.zeros_like(residual)
    direction = apply_precond(residual)
    norm_now = inner_product(residual, direction, weights)
    for iteration in range(ITERS):
        product = lax.map(lambda items: jnp.dot(items[0], items[1].astype(jnp.bfloat16), preferred_element_type=jnp.float32), (stiffness, direction))
        image_vec = assemble(product, face_index)
        step_size = norm_now / inner_product(direction, image_vec, weights)
        solution = solution + step_size * direction
        residual = residual - step_size * image_vec
        precond = apply_precond(residual)
        norm_next = inner_product(residual, precond, weights)
        direction = precond + (norm_next / norm_now) * direction
        norm_now = norm_next
    return (solution, residual, direction)
```

```python
import functools

import jax
import jax.numpy as jnp
from jax import lax
from jax.experimental import pallas as pl
from jax.experimental.pallas import tpu as pltpu
from jax.sharding import PartitionSpec as P

ITERS = 2
MESH = pl.DeviceIdType.MESH
F32 = jnp.float32
BF16 = jnp.bfloat16
NN = (((1,), (0,)), ((), ()))
NT = (((1,), (1,)), ((), ()))
CHUNK = 128


def dot(a, b, dims=NN):
    return lax.dot_general(a, b, dims, preferred_element_type=F32)


def split(a):
    hi = a.astype(BF16)
    return hi, (a - hi.astype(F32)).astype(BF16)


def dot3(a, b, dims=NN):
    (a_hi, a_lo), (b_hi, b_lo) = a, b
    return dot(a_hi, b_hi, dims) + (dot(a_lo, b_hi, dims) + dot(a_hi, b_lo, dims))


def fold(values):
    rows, cols = values.shape
    return jnp.sum(values.reshape(rows // 8, 8, cols), axis=0)


def main_kernel(
    n_group, n_dev,
    loads_hbm, stiff_hbm, inv_hbm, basis_hbm, pos_smem, pos_row, cmap_row, ginv_ref, tbasis_ref, tinv_ref,
    x_out, r_out, d_out,
    loads, stiff, inv, basis, perm_t,
    field, res, dirn, sol, prod, scaled, scaled_lo, plain,
    face_in, basis_f32, basis_bf, basis_in, comb_t, comb,
    ginv_hi, ginv_lo, tb_hi, tb_lo, tbq_hi, tbq_lo, t2_hi, t2_lo, pad_a, pad_b,
    coarse, u_out, u_in, top_in, ts_in, own, own_in, dot_dev, dot_group,
    load_sem, out_sem, face_send, face_recv, basis_send, basis_recv, own_send, own_recv,
    coarse_send, coarse_recv, u_send, u_recv, top_send, top_recv, ts_send, ts_recv,
    dd_send, dd_recv, dg_send, dg_recv,
):
    g = lax.axis_index("group")
    d = lax.axis_index("dev")
    ni, nrhs = loads.shape
    ncon = basis.shape[0]
    face = ni // 4
    per_dev = nrhs // n_dev
    has = [d > 0, d < n_dev - 1, g > 0, g < n_group - 1]
    target = [(g, d - 1), (g, d + 1), (g - 1, d), (g + 1, d)]
    opposite = [1, 0, 3, 2]
    w = [jnp.where(h, 0.5, 1.0).astype(F32) for h in has]

    def dev_peer(i):
        return (g, lax.rem(d + i, n_dev))

    def group_peer(i):
        return (lax.rem(g + i, n_group), d)

    def fetch(src, dst, k):
        return pltpu.make_async_copy(src, dst, load_sem.at[k])

    fetch_loads = fetch(loads_hbm, loads, 0)
    fetch_basis = fetch(basis_hbm, basis, 1)
    fetch_inv = fetch(inv_hbm, inv, 2)
    fetch_stiff = fetch(stiff_hbm, stiff, 3)
    fetch_loads.start()
    fetch_basis.start()
    fetch_inv.start()
    fetch_stiff.start()

    barrier = pltpu.get_barrier_semaphore()

    def greet_dev(i, carry):
        pl.semaphore_signal(barrier, inc=1, device_id=dev_peer(i), device_id_type=MESH)
        return carry

    def greet_group(i, carry):
        pl.semaphore_signal(barrier, inc=1, device_id=group_peer(i), device_id_type=MESH)
        return carry

    lax.fori_loop(1, n_dev, greet_dev, 0)
    lax.fori_loop(1, n_group, greet_group, 0)

    def spread(src_of, buf, k, send, recv, along_dev):
        n, me = (n_dev, d) if along_dev else (n_group, g)
        peer_of = dev_peer if along_dev else group_peer

        def body(i, carry):
            peer = peer_of(i)
            pltpu.make_async_remote_copy(
                src_ref=src_of(peer[1] if along_dev else peer[0]),
                dst_ref=buf.at[k, me],
                send_sem=send.at[k],
                recv_sem=recv.at[k],
                device_id=peer,
                device_id_type=MESH,
            ).start()
            return carry

        lax.fori_loop(1, n, body, 0)

    def all_of(buf, k, send, recv, along_dev):
        n = n_dev if along_dev else n_group
        part = buf.at[k, pl.ds(0, n - 1)]
        return pltpu.make_async_remote_copy(
            src_ref=part, dst_ref=part, send_sem=send.at[k], recv_sem=recv.at[k],
            device_id=dev_peer(1) if along_dev else group_peer(1), device_id_type=MESH,
        )

    def face_copy(src, e, b):
        return pltpu.make_async_remote_copy(
            src_ref=src.at[pl.ds(b * face, face)], dst_ref=face_in.at[e, opposite[b]],
            send_sem=face_send.at[e, b], recv_sem=face_recv.at[e, opposite[b]],
            device_id=target[b], device_id_type=MESH,
        )

    def face_wait(src, e, b):
        return pltpu.make_async_remote_copy(
            src_ref=src.at[pl.ds(b * face, face)], dst_ref=face_in.at[e, b],
            send_sem=face_send.at[e, b], recv_sem=face_recv.at[e, b],
            device_id=target[b], device_id_type=MESH,
        )

    def send_face(src, e, b):
        @pl.when(has[b])
        def _():
            face_copy(src, e, b).start()

    def recv_face(src, e, b):
        @pl.when(has[b])
        def _():
            face_wait(src, e, b).wait_recv()

    def sent_face(src, e, b):
        @pl.when(has[b])
        def _():
            face_copy(src, e, b).wait_send()

    def basis_copy(b):
        return pltpu.make_async_remote_copy(
            src_ref=basis_f32.at[:, pl.ds(b * face, face)], dst_ref=basis_in.at[opposite[b]],
            send_sem=basis_send.at[b], recv_sem=basis_recv.at[opposite[b]],
            device_id=target[b], device_id_type=MESH,
        )

    def basis_wait(b):
        return pltpu.make_async_remote_copy(
            src_ref=basis_f32.at[:, pl.ds(b * face, face)], dst_ref=basis_in.at[b],
            send_sem=basis_send.at[b], recv_sem=basis_recv.at[b],
            device_id=target[b], device_id_type=MESH,
        )

    def own_copy(m, b):
        return pltpu.make_async_remote_copy(
            src_ref=own.at[m], dst_ref=own_in.at[m, opposite[b]],
            send_sem=own_send.at[m, b], recv_sem=own_recv.at[m, opposite[b]],
            device_id=target[b], device_id_type=MESH,
        )

    def own_wait(m, b):
        return pltpu.make_async_remote_copy(
            src_ref=own.at[m], dst_ref=own_in.at[m, b],
            send_sem=own_send.at[m, b], recv_sem=own_recv.at[m, b],
            device_id=target[b], device_id_type=MESH,
        )

    def gather_face(src, dst, b):
        def body(step, carry):
            base = b * face + step * 16
            for j in range(16):
                row = pos_smem[0, base + j]
                dst[pl.ds(base + j, 1), :] = src[pl.ds(row, 1), :]
            return carry

        lax.fori_loop(0, face // 16, body, 0)

    def over_face(b, body, init):
        def step(i, carry):
            return body(pl.ds(pl.multiple_of(b * face + i * CHUNK, CHUNK), CHUNK),
                        pl.ds(pl.multiple_of(i * CHUNK, CHUNK), CHUNK), carry)

        return lax.fori_loop(0, face // CHUNK, step, init)

    def apply(matrix, vector, out, out_type):
        rows = 512 if ni % 512 == 0 else ni

        def body(i, carry):
            at = pl.ds(pl.multiple_of(i * rows, rows), rows)
            out[at, :] = dot(matrix[at, :], vector[...]).astype(out_type)
            return carry

        lax.fori_loop(0, ni // rows, body, 0)

    for b in range(4):
        @pl.when(jnp.logical_not(has[b]))
        def _():
            def zero(e, carry):
                face_in[e, b] = jnp.zeros((face, nrhs), F32)
                return carry

            lax.fori_loop(0, face_in.shape[0], zero, 0)
            for m in range(ITERS + 1):
                own_in[m, b] = jnp.zeros((ncon, nrhs), F32)
            basis_in[b] = jnp.zeros((ncon, face), F32)

    fetch_loads.wait()
    gather_face(loads, field, 0)
    gather_face(loads, field, 1)
    pl.semaphore_wait(barrier, n_dev - 1 + n_group - 1)
    send_face(field, 0, 0)
    send_face(field, 0, 1)
    gather_face(loads, field, 2)
    send_face(field, 0, 2)
    gather_face(loads, field, 3)
    send_face(field, 0, 3)

    def build(i, carry):
        rows = lax.broadcasted_iota(jnp.int32, (CHUNK, ni), 0) + i * CHUNK
        at = pl.ds(pl.multiple_of(i * CHUNK, CHUNK), CHUNK)
        perm_t[at, :] = jnp.where(rows == pos_row[...], 1.0, 0.0).astype(BF16)
        return carry

    lax.fori_loop(0, ni // CHUNK, build, 0)

    select = jnp.where(
        lax.broadcasted_iota(jnp.int32, (ncon, ncon), 0) == cmap_row[...], 1.0, 0.0
    ).astype(BF16)
    fetch_basis.wait()
    ordered = dot(select, basis[...]).astype(BF16)
    width = 512 if ni % 512 == 0 else ni
    for j in range(ni // width):
        block = dot(ordered, perm_t[:, j * width:(j + 1) * width])
        basis_f32[:, j * width:(j + 1) * width] = block
        basis_bf[:, j * width:(j + 1) * width] = block.astype(BF16)
    for b in range(4):
        @pl.when(has[b])
        def _():
            basis_copy(b).start()

    ginv_hi[...], ginv_lo[...] = split(ginv_ref[...])
    topc = tbasis_ref.shape[1]
    pad_a[...] = jnp.zeros_like(pad_a)
    pad_a[0:ncon, 0:topc] = tbasis_ref[...]
    tb_hi[...], tb_lo[...] = split(pad_a[...])
    mark_row = lax.broadcasted_iota(jnp.int32, (64, 128), 0)
    mark_col = lax.broadcasted_iota(jnp.int32, (64, 128), 1)
    marked = jnp.where((mark_row == ncon) & (mark_col == 64), 1.0, pad_a[0:64, :])
    tbq_hi[...], tbq_lo[...] = split(marked)
    pad_b[...] = jnp.zeros_like(pad_b)
    pad_b[0:topc, 0:n_group * topc] = tinv_ref[...]
    t2_hi[...] = jnp.zeros_like(t2_hi)
    t2_lo[...] = jnp.zeros_like(t2_lo)
    for q in range(n_group):
        tinv_t = pad_b[:, (q * topc) // 128 * 128:((q * topc) // 128 + 2) * 128].T
        start = (q * topc) % 128
        hi, lo = split(tinv_t[start:start + topc])
        at = (q // 2) * 128 + (q % 2) * 64
        t2_hi[at:at + topc, :] = hi
        t2_lo[at:at + topc, :] = lo

    for b in range(4):
        recv_face(field, 0, b)

        def add(at, at_in, carry):
            value = field[at, :] + face_in[0, b, at_in, :]
            res[at, :] = value
            scaled[at, :] = (w[b] * value).astype(BF16)
            scaled_lo[at, :] = (w[b] * value - (w[b] * value).astype(BF16).astype(F32)).astype(BF16)
            return carry

        over_face(b, add, 0)

    odd = lax.rem(g, 2) == 1

    def precondition(m, e, before_end):
        own_coarse = dot(basis_bf[...], scaled[...])
        coarse[m, d] = own_coarse
        pad_a[0:ncon, :] = own_coarse
        u_t = dot3(split(pad_a[...].T), (tb_hi[...], tb_lo[...]))
        u_out[m] = u_t.reshape(n_dev, per_dev, 128)
        u_in[m, d] = u_out[m, d]
        spread(lambda p: u_out.at[m, p], u_in, m, u_send, u_recv, True)
        spread(lambda p: coarse.at[m, d], coarse, m, coarse_send, coarse_recv, True)

        apply(perm_t, scaled, plain, BF16)
        exact_coarse = own_coarse + dot(basis_bf[...], scaled_lo[...])

        all_of(u_in, m, u_send, u_recv, True).wait_recv()
        top = jnp.sum(u_in[m], axis=0)
        top_in[m, g] = jnp.where(odd, pltpu.roll(top, 64, 1), top)
        spread(lambda p: top_in.at[m, g], top_in, m, top_send, top_recv, False)

        if m == 0:
            fetch_inv.wait()
        apply(inv, plain, prod, F32)
        for b in range(4):
            gather_face(prod, field, b)
            send_face(field, e, b)

        all_of(top_in, m, top_send, top_recv, False).wait_recv()
        every = top_in[m]
        joined = jnp.concatenate(
            [every[2 * q] + every[2 * q + 1] for q in range(n_group // 2)], axis=1
        )
        ts = dot3(split(joined), (t2_hi[...], t2_lo[...]))
        energy = jnp.sum(ts * top, axis=1, keepdims=True)
        lane = lax.broadcasted_iota(jnp.int32, ts.shape, 1)
        ts_in[m, d] = jnp.where(lane == 64, energy, ts)
        spread(lambda p: ts_in.at[m, d], ts_in, m, ts_send, ts_recv, True)

        total = jnp.zeros((8, nrhs), F32)
        for b in range(4):
            def part(at, at_in, carry):
                return carry + fold(res[at, :] * field[at, :])

            total = total + w[b] * over_face(b, part, jnp.zeros((8, nrhs), F32))

        all_of(coarse, m, coarse_send, coarse_recv, True).wait_recv()
        solved = dot3((ginv_hi[...], ginv_lo[...]), split(coarse[m].reshape(n_dev * ncon, nrhs)))
        k = m
        dot_dev[k, d] = total + fold(exact_coarse * solved)
        spread(lambda p: dot_dev.at[k, d], dot_dev, k, dd_send, dd_recv, True)

        all_of(ts_in, m, ts_send, ts_recv, True).wait_recv()
        upper = dot3((tbq_hi[...], tbq_lo[...]), split(ts_in[m].reshape(nrhs, 128)), NT)
        own[m] = solved + upper[0:ncon]
        for b in range(4):
            @pl.when(has[b])
            def _():
                own_copy(m, b).start()

        all_of(dot_dev, k, dd_send, dd_recv, True).wait_recv()
        row = lax.broadcasted_iota(jnp.int32, (8, nrhs), 0)
        dot_group[k, g] = jnp.sum(dot_dev[k], axis=0) + jnp.where(
            row == 0, upper[ncon:ncon + 1], 0.0
        )
        spread(lambda p: dot_group.at[k, g], dot_group, k, dg_send, dg_recv, False)

        before_end()

        own_hi, own_lo = split(own[m])
        for b in range(4):
            @pl.when(has[b])
            def _():
                own_wait(m, b).wait_recv()

            recv_face(field, e, b)
            in_hi, in_lo = split(own_in[m, b])
            values = jnp.concatenate(
                [own_hi, in_hi, own_lo, in_lo, jnp.zeros((256 - 4 * ncon, nrhs), BF16)], axis=0
            )

            def join(at, at_in, carry):
                prod[at, :] = w[b] * (
                    field[at, :] + face_in[e, b, at_in, :] + dot(comb[at, :], values)
                )
                return carry

            over_face(b, join, 0)

        all_of(dot_group, k, dg_send, dg_recv, False).wait_recv()
        return jnp.sum(jnp.sum(dot_group[k], axis=0), axis=0, keepdims=True)

    def drain(m, e):
        all_of(u_in, m, u_send, u_recv, True).wait_send()
        all_of(coarse, m, coarse_send, coarse_recv, True).wait_send()
        all_of(top_in, m, top_send, top_recv, False).wait_send()
        all_of(ts_in, m, ts_send, ts_recv, True).wait_send()
        all_of(dot_dev, m, dd_send, dd_recv, True).wait_send()
        all_of(dot_group, m, dg_send, dg_recv, False).wait_send()
        for b in range(4):
            @pl.when(has[b])
            def _():
                own_copy(m, b).wait_send()

            sent_face(field, e, b)

    for b in range(4):
        sent_face(field, 0, b)
    pad_a[...] = jnp.zeros_like(pad_a)

    def combine():
        for b in range(4):
            @pl.when(has[b])
            def _():
                basis_wait(b).wait_recv()

            at = slice(b * face, (b + 1) * face)
            comb_t[0:ncon, at] = basis_f32[:, at]
            comb_t[ncon:2 * ncon, at] = basis_in[b]
            comb_t[2 * ncon:3 * ncon, at] = basis_f32[:, at]
            comb_t[3 * ncon:4 * ncon, at] = basis_in[b]
        comb_t[4 * ncon:, :] = jnp.zeros((256 - 4 * ncon, ni), F32)
        for j in range(ni // 128):
            comb[j * 128:(j + 1) * 128, :] = comb_t[:, j * 128:(j + 1) * 128].T.astype(BF16)
        for b in range(4):
            @pl.when(has[b])
            def _():
                basis_copy(b).wait_send()

    norm = precondition(0, 1, combine)

    def first(i, carry):
        at = pl.ds(pl.multiple_of(i * CHUNK, CHUNK), CHUNK)
        value = prod[at, :]
        dirn[at, :] = value
        scaled[at, :] = value.astype(BF16)
        return carry

    lax.fori_loop(0, ni // CHUNK, first, 0)
    drain(0, 1)

    fetch_stiff.wait()
    for it in range(ITERS):
        e = 2 + 2 * it
        k = ITERS + 1 + it
        apply(perm_t, scaled, plain, BF16)
        apply(stiff, plain, prod, F32)
        for b in range(4):
            gather_face(prod, field, b)
            send_face(field, e, b)

        def part(i, carry):
            at = pl.ds(pl.multiple_of(i * CHUNK, CHUNK), CHUNK)
            return carry + fold(dirn[at, :] * field[at, :])

        dot_dev[k, d] = lax.fori_loop(0, ni // CHUNK, part, jnp.zeros((8, nrhs), F32))
        spread(lambda p: dot_dev.at[k, d], dot_dev, k, dd_send, dd_recv, True)
        all_of(dot_dev, k, dd_send, dd_recv, True).wait_recv()
        dot_group[k, g] = jnp.sum(dot_dev[k], axis=0)
        spread(lambda p: dot_group.at[k, g], dot_group, k, dg_send, dg_recv, False)
        all_of(dot_group, k, dg_send, dg_recv, False).wait_recv()
        curvature = jnp.sum(jnp.sum(dot_group[k], axis=0), axis=0, keepdims=True)
        step_size = norm / curvature

        for b in range(4):
            recv_face(field, e, b)

            def update(at, at_in, carry):
                image = field[at, :] + face_in[e, b, at_in, :]
                value = res[at, :] - step_size * image
                res[at, :] = value
                weighted = w[b] * value
                rounded = weighted.astype(BF16)
                scaled[at, :] = rounded
                scaled_lo[at, :] = (weighted - rounded.astype(F32)).astype(BF16)
                return carry

            over_face(b, update, 0)
        for b in range(4):
            sent_face(field, e, b)

        def after(it=it, step_size=step_size):
            def body(i, carry):
                at = pl.ds(pl.multiple_of(i * CHUNK, CHUNK), CHUNK)
                add = step_size * dirn[at, :]
                sol[at, :] = add if it == 0 else sol[at, :] + add
                return carry

            lax.fori_loop(0, ni // CHUNK, body, 0)
            if it == ITERS - 1:
                pltpu.make_async_copy(sol, x_out, out_sem.at[0]).start()
                pltpu.make_async_copy(res, r_out, out_sem.at[1]).start()

        norm_next = precondition(it + 1, e + 1, after)
        ratio = norm_next / norm

        def turn(i, carry):
            at = pl.ds(pl.multiple_of(i * CHUNK, CHUNK), CHUNK)
            value = prod[at, :] + ratio * dirn[at, :]
            dirn[at, :] = value
            scaled[at, :] = value.astype(BF16)
            return carry

        lax.fori_loop(0, ni // CHUNK, turn, 0)
        norm = norm_next
        if it == ITERS - 1:
            pltpu.make_async_copy(dirn, d_out, out_sem.at[2]).start()
        all_of(dot_dev, k, dd_send, dd_recv, True).wait_send()
        all_of(dot_group, k, dg_send, dg_recv, False).wait_send()
        drain(it + 1, e + 1)

    pltpu.make_async_copy(sol, x_out, out_sem.at[0]).wait()
    pltpu.make_async_copy(res, r_out, out_sem.at[1]).wait()
    pltpu.make_async_copy(dirn, d_out, out_sem.at[2]).wait()


def reorder_kernel(pos_smem, x_in, r_in, d_in, x_out, r_out, d_out):
    def body(step, carry):
        for j in range(8):
            at = step * 8 + j
            row = pos_smem[0, at]
            x_out[pl.ds(row, 1), :] = x_in[pl.ds(at, 1), :]
            r_out[pl.ds(row, 1), :] = r_in[pl.ds(at, 1), :]
            d_out[pl.ds(row, 1), :] = d_in[pl.ds(at, 1), :]
        return carry

    lax.fori_loop(0, x_in.shape[0] // 8, body, 0)


def local(
    n_group, n_dev,
    applied_loads, stiffness, local_inverse, coarse_basis, face_index, coarse_map, group_inverse, top_basis, top_inverse,
):
    ni, nrhs = applied_loads.shape[1:]
    ncon = coarse_basis.shape[1]
    topc = top_basis.shape[1]
    face = ni // 4
    per_dev = nrhs // n_dev
    uses = ITERS + 1
    dots = 2 * ITERS + 1
    exchanges = 2 * ITERS + 2
    top_cols = n_group // 2 * 128
    top_pad = (n_group * topc + 127) // 128 * 128 + 128
    vmem = pl.BlockSpec(memory_space=pltpu.VMEM)
    smem = pl.BlockSpec(memory_space=pltpu.SMEM)
    hbm = pl.BlockSpec(memory_space=pl.ANY)
    field = jax.ShapeDtypeStruct((ni, nrhs), F32)
    dma = pltpu.SemaphoreType.DMA
    scratch = [
        pltpu.VMEM((ni, nrhs), F32), pltpu.VMEM((ni, ni), BF16), pltpu.VMEM((ni, ni), BF16),
        pltpu.VMEM((ncon, ni), BF16), pltpu.VMEM((ni, ni), BF16),
        pltpu.VMEM((ni, nrhs), F32), pltpu.VMEM((ni, nrhs), F32), pltpu.VMEM((ni, nrhs), F32),
        pltpu.VMEM((ni, nrhs), F32), pltpu.VMEM((ni, nrhs), F32),
        pltpu.VMEM((ni, nrhs), BF16), pltpu.VMEM((ni, nrhs), BF16), pltpu.VMEM((ni, nrhs), BF16),
        pltpu.VMEM((exchanges, 4, face, nrhs), F32),
        pltpu.VMEM((ncon, ni), F32), pltpu.VMEM((ncon, ni), BF16), pltpu.VMEM((4, ncon, face), F32),
        pltpu.VMEM((256, ni), F32), pltpu.VMEM((ni, 256), BF16),
        pltpu.VMEM((ncon, n_dev * ncon), BF16), pltpu.VMEM((ncon, n_dev * ncon), BF16),
        pltpu.VMEM((128, 128), BF16), pltpu.VMEM((128, 128), BF16),
        pltpu.VMEM((64, 128), BF16), pltpu.VMEM((64, 128), BF16),
        pltpu.VMEM((top_cols, 128), BF16), pltpu.VMEM((top_cols, 128), BF16),
        pltpu.VMEM((128, 128), F32), pltpu.VMEM((128, top_pad), F32),
        pltpu.VMEM((uses, n_dev, ncon, nrhs), F32),
        pltpu.VMEM((uses, n_dev, per_dev, 128), F32), pltpu.VMEM((uses, n_dev, per_dev, 128), F32),
        pltpu.VMEM((uses, n_group, per_dev, 128), F32),
        pltpu.VMEM((uses, n_dev, per_dev, 128), F32),
        pltpu.VMEM((uses, ncon, nrhs), F32), pltpu.VMEM((uses, 4, ncon, nrhs), F32),
        pltpu.VMEM((dots, n_dev, 8, nrhs), F32), pltpu.VMEM((dots, n_group, 8, nrhs), F32),
        dma((4,)), dma((3,)),
        dma((exchanges, 4)), dma((exchanges, 4)), dma((4,)), dma((4,)), dma((uses, 4)), dma((uses, 4)),
        dma((uses,)), dma((uses,)), dma((uses,)), dma((uses,)),
        dma((uses,)), dma((uses,)), dma((uses,)), dma((uses,)),
        dma((dots,)), dma((dots,)), dma((dots,)), dma((dots,)),
    ]
    x, r, dirn = pl.pallas_call(
        functools.partial(main_kernel, n_group, n_dev),
        out_shape=[field] * 3,
        in_specs=[hbm, hbm, hbm, hbm, smem, vmem, vmem, vmem, vmem, vmem],
        out_specs=[hbm] * 3,
        scratch_shapes=scratch,
        compiler_params=pltpu.CompilerParams(
            collective_id=0, has_side_effects=True, vmem_limit_bytes=56 * 2**20
        ),
        cost_estimate=pl.CostEstimate(
            flops=18 * ni * ni * nrhs, bytes_accessed=4 * ni * ni + 24 * ni * nrhs, transcendentals=0
        ),
        name="pcg",
    )(
        applied_loads[0], stiffness[0], local_inverse[0], coarse_basis[0],
        face_index, face_index, coarse_map, group_inverse, top_basis, top_inverse,
    )
    x, r, dirn = pl.pallas_call(
        reorder_kernel,
        out_shape=[field] * 3,
        in_specs=[smem, vmem, vmem, vmem],
        out_specs=[vmem] * 3,
        compiler_params=pltpu.CompilerParams(vmem_limit_bytes=32 * 2**20),
        cost_estimate=pl.CostEstimate(flops=0, bytes_accessed=24 * ni * nrhs, transcendentals=0),
        name="to_subdomain_order",
    )(face_index, x, r, dirn)
    return x[None], r[None], dirn[None]


def solution(mesh):
    both = ("group", "dev")
    return jax.shard_map(
        functools.partial(local, mesh.shape["group"], mesh.shape["dev"]),
        mesh=mesh,
        in_specs=(
            P(both, None, None), P(both, None, None), P(both, None, None), P(both, None, None),
            P(both, None), P(both, None), P(both, None), P(both, None), P("group", None),
        ),
        out_specs=(P(both, None, None),) * 3,
        check_vma=False,
    )
```

```python
import functools

import jax
import jax.numpy as jnp
from jax import lax
from jax.experimental import pallas as pl
from jax.experimental.pallas import tpu as pltpu
from jax.sharding import PartitionSpec as P

ITERS = 2
MESH = pl.DeviceIdType.MESH
F32 = jnp.float32
BF16 = jnp.bfloat16
NN = (((1,), (0,)), ((), ()))
NT = (((1,), (1,)), ((), ()))
CHUNK = 128
ROWS = 512


def dot(a, b, dims=NN):
    return lax.dot_general(a, b, dims, preferred_element_type=F32)


def split(a):
    hi = a.astype(BF16)
    return hi, (a - hi.astype(F32)).astype(BF16)


def dot3(a, b, dims=NN):
    (a_hi, a_lo), (b_hi, b_lo) = a, b
    return dot(a_hi, b_hi, dims) + (dot(a_lo, b_hi, dims) + dot(a_hi, b_lo, dims))


def fold(values):
    rows, cols = values.shape
    return jnp.sum(values.reshape(rows // 8, 8, cols), axis=0)


def main_kernel(
    n_group, n_dev,
    loads_hbm, stiff_hbm, inv_hbm, basis_hbm, pos_smem, pos_row, cmap_row, ginv_ref, tbasis_ref, tinv_ref,
    x_out, r_out, d_out, one_out,
    loads, stiff, inv, basis, perm_t, place_vec, place_smem,
    field, local_part, res, dirn, sol, prod, weighted, scaled, scaled_lo, plain,
    face_in, basis_f32, basis_in, basis_all, comb_t, comb,
    ginv_hi, ginv_lo, tb_all, tb_all_hi, tb_all_lo, t2_hi, t2_lo, tinv_all, turned,
    tb_own, tb_in, tinv_own, tinv_in, upper,
    parts, parts_in, coarse, u_out, u_in, top_in, ts_in, solved_own, solved_in,
    group_now, top_now, step_now, step_cols, norm_now, dot_dev, dot_group, curv_dev, curv_group,
    load_sem, out_sem, face_send, face_recv, basis_send, basis_recv, tb_send, tb_recv,
    tinv_send, tinv_recv, parts_send, parts_recv, solved_send, solved_recv,
    coarse_send, coarse_recv, u_send, u_recv, top_send, top_recv, ts_send, ts_recv,
    dd_send, dd_recv, dg_send, dg_recv, cd_send, cd_recv, cg_send, cg_recv,
):
    g = lax.axis_index("group")
    d = lax.axis_index("dev")
    ni, nrhs = loads.shape
    ncon = basis.shape[0]
    topc = tbasis_ref.shape[1]
    face = ni // 4
    per_dev = nrhs // n_dev
    has = [d > 0, d < n_dev - 1, g > 0, g < n_group - 1]
    target = [(g, d - 1), (g, d + 1), (g - 1, d), (g + 1, d)]
    opposite = [1, 0, 3, 2]
    w = [jnp.where(h, 0.5, 1.0).astype(F32) for h in has]

    def weight_of(b):
        return jnp.where(b == 0, w[0], jnp.where(b == 1, w[1], jnp.where(b == 2, w[2], w[3])))

    def dev_peer(i):
        return (g, lax.rem(d + i, n_dev))

    def group_peer(i):
        return (lax.rem(g + i, n_group), d)

    def fetch(src, dst, k):
        return pltpu.make_async_copy(src, dst, load_sem.at[k])

    fetch_loads = fetch(loads_hbm, loads, 0)
    fetch_basis = fetch(basis_hbm, basis, 1)
    fetch_inv = fetch(inv_hbm, inv, 2)
    fetch_stiff = fetch(stiff_hbm, stiff, 3)
    fetch_basis.start()
    fetch_loads.start()
    one_out[...] = jnp.ones_like(one_out)

    barrier = pltpu.get_barrier_semaphore()

    def greet_dev(i, carry):
        pl.semaphore_signal(barrier, inc=1, device_id=dev_peer(i), device_id_type=MESH)
        return carry

    def greet_group(i, carry):
        pl.semaphore_signal(barrier, inc=1, device_id=group_peer(i), device_id_type=MESH)
        return carry

    lax.fori_loop(1, n_dev, greet_dev, 0)
    lax.fori_loop(1, n_group, greet_group, 0)

    def spread(src_of, buf, k, send, recv, along_dev):
        n, me = (n_dev, d) if along_dev else (n_group, g)
        peer_of = dev_peer if along_dev else group_peer

        def body(i, carry):
            peer = peer_of(i)
            pltpu.make_async_remote_copy(
                src_ref=src_of(peer[1] if along_dev else peer[0]),
                dst_ref=buf.at[k, me],
                send_sem=send.at[k],
                recv_sem=recv.at[k],
                device_id=peer,
                device_id_type=MESH,
            ).start()
            return carry

        lax.fori_loop(1, n, body, 0)

    def all_of(buf, k, send, recv, along_dev):
        n = n_dev if along_dev else n_group
        part = buf.at[k, pl.ds(0, n - 1)]
        return pltpu.make_async_remote_copy(
            src_ref=part, dst_ref=part, send_sem=send.at[k], recv_sem=recv.at[k],
            device_id=dev_peer(1) if along_dev else group_peer(1), device_id_type=MESH,
        )

    def neighbour_copy(src, dst, send, recv, b):
        return pltpu.make_async_remote_copy(
            src_ref=src, dst_ref=dst, send_sem=send, recv_sem=recv,
            device_id=target[b], device_id_type=MESH,
        )

    def face_copy(src, e, b, slot):
        return neighbour_copy(
            src.at[pl.ds(b * face, face)], face_in.at[e, slot], face_send.at[e, b], face_recv.at[e, slot], b
        )

    def basis_copy(b, slot):
        return neighbour_copy(
            basis_f32.at[:, pl.ds(b * face, face)], basis_in.at[slot], basis_send.at[b], basis_recv.at[slot], b
        )

    def tb_copy(b, slot):
        return neighbour_copy(tb_own, tb_in.at[slot], tb_send.at[b], tb_recv.at[slot], b)

    def tinv_copy(b, slot):
        return neighbour_copy(tinv_own, tinv_in.at[slot - 2], tinv_send.at[b - 2], tinv_recv.at[slot - 2], b)

    def parts_copy(m, b, slot):
        return neighbour_copy(
            parts.at[m, pl.ds((b + 1) * ncon, ncon)], parts_in.at[m, slot],
            parts_send.at[m, b], parts_recv.at[m, slot], b,
        )

    def solved_copy(m, b, slot):
        return neighbour_copy(
            solved_own.at[m], solved_in.at[m, slot], solved_send.at[m, b], solved_recv.at[m, slot], b
        )

    def each_face(body, faces=(0, 1, 2, 3)):
        for b in faces:
            @pl.when(has[b])
            def _():
                body(b)

    def pick_rows(index, src, dst):
        def body(step, carry):
            base = step * 32
            for j in range(32):
                dst[pl.ds(base + j, 1), :] = src[pl.ds(index[0, base + j], 1), :]
            return carry

        lax.fori_loop(0, ni // 32, body, 0)

    def to_faces(src, dst):
        pick_rows(pos_smem, src, dst)

    def from_faces(src, dst):
        pick_rows(place_smem, src, dst)

    def over_chunks(body, init=0):
        per_face = face // CHUNK

        def step(i, carry):
            b = i // per_face
            at_in = pl.multiple_of((i - b * per_face) * CHUNK, CHUNK)
            return body(pl.ds(pl.multiple_of(i * CHUNK, CHUNK), CHUNK), b, pl.ds(at_in, CHUNK), carry)

        return lax.fori_loop(0, ni // CHUNK, step, init)

    def apply(matrix, vector, out, out_type):
        rows = ROWS if ni % ROWS == 0 else ni

        def body(i, carry):
            at = pl.ds(pl.multiple_of(i * rows, rows), rows)
            out[at, :] = dot(matrix[at, :], vector[...]).astype(out_type)
            return carry

        lax.fori_loop(0, ni // rows, body, 0)

    for b in range(4):
        @pl.when(jnp.logical_not(has[b]))
        def _():
            def zero_faces(e, carry):
                face_in[e, b] = jnp.zeros((face, nrhs), F32)
                return carry

            def zero_parts(m, carry):
                parts_in[m, b] = jnp.zeros((ncon, nrhs), F32)
                solved_in[m, b] = jnp.zeros((ncon, nrhs), F32)
                return carry

            lax.fori_loop(0, face_in.shape[0], zero_faces, 0)
            lax.fori_loop(0, ITERS + 1, zero_parts, 0)
            basis_in[b] = jnp.zeros((ncon, face), F32)
            tb_in[b] = jnp.zeros(tb_own.shape, F32)
            if b >= 2:
                tinv_in[b - 2] = jnp.zeros(tinv_own.shape, F32)

    spots = (
        lax.broadcasted_iota(jnp.int32, place_vec.shape, 0) * 128
        + lax.broadcasted_iota(jnp.int32, place_vec.shape, 1)
    )

    def invert(step, found):
        for j in range(32):
            k = step * 32 + j
            found = jnp.where(spots == pos_smem[0, k], k, found)
        return found

    place_vec[...] = lax.fori_loop(0, ni // 32, invert, jnp.zeros(place_vec.shape, jnp.int32))
    place_copies = [
        pltpu.make_async_copy(
            place_vec.at[pl.ds(i, 1)], place_smem.at[:, pl.ds(i * 128, 128)], load_sem.at[4 + i]
        )
        for i in range(ni // 128)
    ]
    for copy in place_copies:
        copy.start()

    select = jnp.where(
        lax.broadcasted_iota(jnp.int32, (ncon, ncon), 0) == cmap_row[...], 1.0, 0.0
    ).astype(BF16)
    fetch_basis.wait()
    fetch_loads.wait()
    fetch_inv.start()
    fetch_stiff.start()
    tb_own[...] = jnp.zeros_like(tb_own)
    tb_own[:, 0:topc] = tbasis_ref[...]
    tinv_own[...] = tinv_ref[...]

    def turn_basis(j, carry):
        at = pl.ds(pl.multiple_of(j * 128, 128), 128)
        block = dot(select, basis[:, at])
        prod[at, :] = jnp.concatenate([block, jnp.zeros((128 - ncon, 128), F32)], axis=0).T
        return carry

    lax.fori_loop(0, ni // 128, turn_basis, 0)
    to_faces(prod, local_part)

    def turn_back(j, carry):
        at = pl.ds(pl.multiple_of(j * 128, 128), 128)
        basis_f32[:, at] = local_part[at, :].T[0:ncon]
        return carry

    lax.fori_loop(0, ni // 128, turn_back, 0)
    pl.semaphore_wait(barrier, n_dev - 1 + n_group - 1)
    each_face(lambda b: basis_copy(b, opposite[b]).start())
    each_face(lambda b: tb_copy(b, opposite[b]).start())
    to_faces(loads, field)
    each_face(lambda b: face_copy(field, 0, b, opposite[b]).start())
    each_face(lambda b: tinv_copy(b, opposite[b]).start(), (2, 3))

    def build(i, carry):
        rows = lax.broadcasted_iota(jnp.int32, (64, ni), 0) + i * 64
        at = pl.ds(pl.multiple_of(i * 64, 64), 64)
        perm_t[at, :] = jnp.where(rows == pos_row[...], 1.0, 0.0).astype(BF16)
        return carry

    lax.fori_loop(0, ni // 64, build, 0)

    def clear(at, b, at_in, carry):
        zero = jnp.zeros((CHUNK, nrhs), F32)
        res[at, :] = zero
        dirn[at, :] = zero
        sol[at, :] = zero
        return carry

    over_chunks(clear)
    group_now[...] = jnp.zeros_like(group_now)
    top_now[...] = jnp.zeros_like(top_now)
    step_now[...] = jnp.full(step_now.shape, -1.0, F32)
    norm_now[...] = jnp.ones_like(norm_now)
    ginv_hi[...], ginv_lo[...] = split(ginv_ref[...])

    tb_all[...] = jnp.zeros_like(tb_all)
    each_face(lambda b: tb_copy(b, b).wait_recv())
    tb_all[0:ncon, 0:128] = tb_own[...]
    tb_all[ncon:2 * ncon, 0:128] = tb_in[0]
    tb_all[2 * ncon:3 * ncon, 0:128] = tb_in[1]
    tb_all[3 * ncon:4 * ncon, 128:256] = tb_in[2]
    tb_all[4 * ncon:5 * ncon, 128:256] = pltpu.roll(tb_in[3], 64, 1)
    tb_all[5 * ncon:5 * ncon + 8, 0:128] = jnp.where(
        (lax.broadcasted_iota(jnp.int32, (8, 128), 0) == 0)
        & (lax.broadcasted_iota(jnp.int32, (8, 128), 1) == 64), 1.0, 0.0,
    ).astype(F32)
    tb_all_hi[...], tb_all_lo[...] = split(tb_all[...])
    for copy in place_copies:
        copy.wait()

    basis_all[...] = jnp.zeros_like(basis_all)
    basis_all[0:ncon, :] = basis_f32[...].astype(BF16)
    each_face(lambda b: basis_copy(b, b).wait_recv())
    for b in range(4):
        basis_all[(b + 1) * ncon:(b + 2) * ncon, b * face:(b + 1) * face] = basis_in[b].astype(BF16)

    def set_up_top():
        tinv_all[...] = jnp.zeros_like(tinv_all)
        cols = n_group * topc
        tinv_all[0:topc, 0:cols] = tinv_own[...]
        each_face(lambda b: tinv_copy(b, b).wait_recv(), (2, 3))
        tinv_all[128:128 + topc, 0:cols] = tinv_in[0]
        tinv_all[192:192 + topc, 0:cols] = tinv_in[1]

        def turn_over(j, carry):
            at = pl.ds(pl.multiple_of(j * 128, 128), 128)
            turned[at, :] = tinv_all[:, at].T
            return carry

        lax.fori_loop(0, turned.shape[0] // 128, turn_over, 0)
        t2_hi[...] = jnp.zeros_like(t2_hi)
        t2_lo[...] = jnp.zeros_like(t2_lo)

        def place(q, carry):
            hi, lo = split(turned[pl.ds(pl.multiple_of(q * topc, 16), topc), :])
            at = pl.ds(pl.multiple_of(q * 64, 64), topc)
            t2_hi[at, :] = hi
            t2_lo[at, :] = lo
            return carry

        lax.fori_loop(0, n_group, place, 0)

    def combine():
        for b in range(4):
            at = slice(b * face, (b + 1) * face)
            comb_t[0:ncon, at] = basis_f32[:, at]
            comb_t[ncon:2 * ncon, at] = basis_in[b]
            comb_t[2 * ncon:3 * ncon, at] = basis_f32[:, at]
            comb_t[3 * ncon:4 * ncon, at] = basis_in[b]
        comb_t[4 * ncon:, :] = jnp.zeros((256 - 4 * ncon, ni), F32)

        def turn_over(j, carry):
            at = pl.ds(pl.multiple_of(j * 128, 128), 128)
            comb[at, :] = comb_t[:, at].T.astype(BF16)
            return carry

        lax.fori_loop(0, ni // 128, turn_over, 0)

    odd = lax.rem(g, 2) == 1
    n_pairs = n_group // 2

    def total(buf, k):
        return jnp.sum(jnp.sum(buf[k], axis=0), axis=0, keepdims=True)

    def inner_of_plain():
        return over_chunks(
            lambda at, b, at_in, c: c + fold(plain[at, :].astype(F32) * prod[at, :]), jnp.zeros((8, nrhs), F32)
        )

    def iteration(it, carry):
        later = it > 0

        @pl.when(later)
        def _():
            apply(perm_t, scaled, plain, BF16)

            @pl.when(it == 1)
            def _():
                fetch_stiff.wait()

            apply(stiff, plain, prod, F32)
            curv_dev[it, d] = inner_of_plain()
            spread(lambda p: curv_dev.at[it, d], curv_dev, it, cd_send, cd_recv, True)
            to_faces(prod, field)

        def halves(at, b, at_in, c):
            hi, lo = split(weight_of(b) * field[at, :])
            scaled[at, :] = hi
            scaled_lo[at, :] = lo
            return c

        over_chunks(halves)
        shares = dot(basis_all[...], scaled[...]) + dot(basis_all[...], scaled_lo[...])
        parts[it] = shares
        u_t = dot3(split(shares.T), (tb_all_hi[...], tb_all_lo[...]))
        u_out[it, :, 0] = u_t[:, 0:128].reshape(n_dev, per_dev, 128)
        u_out[it, :, 1] = u_t[:, 128:256].reshape(n_dev, per_dev, 128)
        u_in[it, d] = u_out[it, d]
        spread(lambda p: u_out.at[it, p], u_in, it, u_send, u_recv, True)
        each_face(lambda b: parts_copy(it, b, opposite[b]).start())

        @pl.when(later)
        def _():
            each_face(lambda b: face_copy(field, 2 * it, b, opposite[b]).start())

        @pl.when(it == 0)
        def _():
            set_up_top()

        each_face(lambda b: parts_copy(it, b, b).wait_recv())
        own_coarse = parts[it, 0:ncon] + (
            (parts_in[it, 0] + parts_in[it, 1]) + (parts_in[it, 2] + parts_in[it, 3])
        )
        coarse[it, d] = own_coarse
        spread(lambda p: coarse.at[it, d], coarse, it, coarse_send, coarse_recv, True)

        @pl.when(later)
        def _():
            all_of(curv_dev, it, cd_send, cd_recv, True).wait_recv()
            curv_group[it, g] = jnp.sum(curv_dev[it], axis=0)
            spread(lambda p: curv_group.at[it, g], curv_group, it, cg_send, cg_recv, False)

        all_of(u_in, it, u_send, u_recv, True).wait_recv()
        own_tile = jnp.sum(u_in[it, :, 0], axis=0)
        side_tile = jnp.sum(u_in[it, :, 1], axis=0)
        lane = lax.broadcasted_iota(jnp.int32, own_tile.shape, 1)
        keep = jnp.where(odd, lane, 127 - lane) < 64
        top_in[it, g, 0] = jnp.where(odd, pltpu.roll(own_tile, 64, 1), own_tile) + jnp.where(
            keep, side_tile, 0.0
        )
        top_in[it, g, 1] = pltpu.roll(jnp.where(keep, 0.0, side_tile), 64, 1)
        spread(lambda p: top_in.at[it, g], top_in, it, top_send, top_recv, False)

        @pl.when(it == 0)
        def _():
            combine()

        @pl.when(later)
        def _():
            @pl.when(it == 1)
            def _():
                all_of(dot_group, 0, dg_send, dg_recv, False).wait_recv()
                norm_now[...] = total(dot_group, 0)

            all_of(curv_group, it, cg_send, cg_recv, False).wait_recv()
            step_now[...] = norm_now[...] / total(curv_group, it)

        step_size = step_now[...]
        step_cols[...] = jnp.broadcast_to(step_size, step_cols.shape).T
        step_col = step_cols[pl.ds(pl.multiple_of(d * per_dev, per_dev), per_dev), :]

        all_of(top_in, it, top_send, top_recv, False).wait_recv()
        every = top_in[it]
        pairs = []
        for p in range(n_pairs):
            pair = every[2 * p, 0] + every[2 * p + 1, 0]
            if p > 0:
                pair = pair + every[2 * p - 1, 1]
            if p < n_pairs - 1:
                pair = pair + every[2 * p + 2, 1]
            pairs.append(top_now[:, p * 128:(p + 1) * 128] - step_col * pair)
        top_next = jnp.concatenate(pairs, axis=1)
        top_now[...] = top_next
        ts = dot3(split(top_next), (t2_hi[...], t2_lo[...]))
        own_pair = top_now[:, pl.ds(pl.multiple_of(g // 2 * 128, 128), 128)]
        own_top = jnp.where(odd, pltpu.roll(own_pair, 64, 1), own_pair)
        top_energy = jnp.sum(jnp.where(lane < topc, ts[:, 0:128] * own_top, 0.0), axis=1, keepdims=True)
        ts_in[it, d, 0] = jnp.where(lane == 64, top_energy, ts[:, 0:128])
        ts_in[it, d, 1] = ts[:, 128:256]
        spread(lambda p: ts_in.at[it, d], ts_in, it, ts_send, ts_recv, True)

        each_face(lambda b: face_copy(field, 2 * it, b, b).wait_recv())

        def update(at, b, at_in, c):
            value = res[at, :] - step_size * (field[at, :] + face_in[2 * it, b, at_in, :])
            res[at, :] = value
            scaled[at, :] = (weight_of(b) * value).astype(BF16)
            return c

        over_chunks(update)

        apply(perm_t, scaled, plain, BF16)

        @pl.when(it == 0)
        def _():
            fetch_inv.wait()

        apply(inv, plain, prod, F32)

        all_of(coarse, it, coarse_send, coarse_recv, True).wait_recv()
        group_next = group_now[...] - step_size * coarse[it].reshape(n_dev * ncon, nrhs)
        group_now[...] = group_next
        solved = dot3((ginv_hi[...], ginv_lo[...]), split(group_next))
        solved_own[it] = solved
        each_face(lambda b: solved_copy(it, b, opposite[b]).start())

        energy = inner_of_plain()
        own_coarse_now = group_now[pl.ds(pl.multiple_of(d * ncon, 16), ncon), :]
        dot_dev[it, d] = energy + fold(own_coarse_now * solved)
        spread(lambda p: dot_dev.at[it, d], dot_dev, it, dd_send, dd_recv, True)
        to_faces(prod, local_part)
        each_face(lambda b: face_copy(local_part, 2 * it + 1, b, opposite[b]).start())

        def advance(at, b, at_in, c):
            sol[at, :] = sol[at, :] + step_size * dirn[at, :]
            return c

        over_chunks(advance)

        @pl.when(it == ITERS)
        def _():
            from_faces(sol, loads)
            pltpu.make_async_copy(loads, x_out, out_sem.at[0]).start()
            from_faces(res, weighted)
            pltpu.make_async_copy(weighted, r_out, out_sem.at[1]).start()

        all_of(ts_in, it, ts_send, ts_recv, True).wait_recv()
        ts_all = jnp.concatenate(
            [ts_in[it, :, 0].reshape(nrhs, 128), ts_in[it, :, 1].reshape(nrhs, 128)], axis=1
        )
        upper[...] = dot3((tb_all_hi[...], tb_all_lo[...]), split(ts_all), NT)

        all_of(dot_dev, it, dd_send, dd_recv, True).wait_recv()
        line = lax.broadcasted_iota(jnp.int32, (8, nrhs), 0)
        dot_group[it, g] = jnp.sum(dot_dev[it], axis=0) + jnp.where(
            line == 0, upper[5 * ncon:5 * ncon + 1, :], 0.0
        )
        spread(lambda p: dot_group.at[it, g], dot_group, it, dg_send, dg_recv, False)

        own_hi, own_lo = split(solved + upper[0:ncon, :])
        each_face(lambda b: solved_copy(it, b, b).wait_recv())
        each_face(lambda b: face_copy(local_part, 2 * it + 1, b, b).wait_recv())

        def join(b, c):
            above = upper[pl.ds(pl.multiple_of((b + 1) * ncon, 16), ncon), :]
            in_hi, in_lo = split(solved_in[it, b] + above)
            values = jnp.concatenate(
                [own_hi, in_hi, own_lo, in_lo, jnp.zeros((256 - 4 * ncon, nrhs), BF16)], axis=0
            )
            at = pl.ds(pl.multiple_of(b * face, face), face)
            prod[at, :] = weight_of(b) * (
                local_part[at, :] + face_in[2 * it + 1, b] + dot(comb[at, :], values)
            )
            return c

        lax.fori_loop(0, 4, join, 0)

        all_of(u_in, it, u_send, u_recv, True).wait_send()
        all_of(coarse, it, coarse_send, coarse_recv, True).wait_send()
        all_of(top_in, it, top_send, top_recv, False).wait_send()
        all_of(ts_in, it, ts_send, ts_recv, True).wait_send()
        all_of(dot_dev, it, dd_send, dd_recv, True).wait_send()

        def left(b):
            face_copy(field, 2 * it, b, opposite[b]).wait_send()
            face_copy(local_part, 2 * it + 1, b, opposite[b]).wait_send()
            parts_copy(it, b, opposite[b]).wait_send()
            solved_copy(it, b, opposite[b]).wait_send()

        each_face(left)

        @pl.when(later)
        def _():
            all_of(curv_dev, it, cd_send, cd_recv, True).wait_send()
            all_of(curv_group, it, cg_send, cg_recv, False).wait_send()
            all_of(dot_group, it, dg_send, dg_recv, False).wait_recv()
            norm_next = total(dot_group, it)
            step_now[...] = norm_next / norm_now[...]
            norm_now[...] = norm_next

        ratio = step_now[...]

        def turn(at, b, at_in, c):
            value = prod[at, :] + ratio * dirn[at, :]
            dirn[at, :] = value
            scaled[at, :] = value.astype(BF16)
            return c

        over_chunks(turn)
        return carry

    lax.fori_loop(0, ITERS + 1, iteration, 0)

    from_faces(dirn, prod)
    store = pltpu.make_async_copy(prod, d_out, out_sem.at[2])
    store.start()
    for m in range(ITERS + 1):
        all_of(dot_group, m, dg_send, dg_recv, False).wait_send()
    each_face(lambda b: basis_copy(b, opposite[b]).wait_send())
    each_face(lambda b: tb_copy(b, opposite[b]).wait_send())
    each_face(lambda b: tinv_copy(b, opposite[b]).wait_send(), (2, 3))
    pltpu.make_async_copy(loads, x_out, out_sem.at[0]).wait()
    pltpu.make_async_copy(weighted, r_out, out_sem.at[1]).wait()
    store.wait()


def local(
    n_group, n_dev,
    applied_loads, stiffness, local_inverse, coarse_basis, face_index, coarse_map, group_inverse, top_basis, top_inverse,
):
    ni, nrhs = applied_loads.shape[1:]
    ncon = coarse_basis.shape[1]
    topc = top_basis.shape[1]
    face = ni // 4
    per_dev = nrhs // n_dev
    uses = ITERS + 1
    exchanges = 2 * uses
    top_rows = n_group * 64
    top_pad = (n_group * topc + 127) // 128 * 128
    vmem = pl.BlockSpec(memory_space=pltpu.VMEM)
    smem = pl.BlockSpec(memory_space=pltpu.SMEM)
    hbm = pl.BlockSpec(memory_space=pl.ANY)
    field = jax.ShapeDtypeStruct((ni, nrhs), F32)
    dma = pltpu.SemaphoreType.DMA

    def f32(*shape):
        return pltpu.VMEM(shape, F32)

    def bf16(*shape):
        return pltpu.VMEM(shape, BF16)

    scratch = [
        f32(ni, nrhs), bf16(ni, ni), bf16(ni, ni), bf16(ncon, ni), bf16(ni, ni),
        pltpu.VMEM((ni // 128, 128), jnp.int32), pltpu.SMEM((1, ni), jnp.int32),
        f32(ni, nrhs),
        f32(ni, nrhs), f32(ni, nrhs), f32(ni, nrhs), f32(ni, nrhs), f32(ni, nrhs), f32(ni, nrhs),
        bf16(ni, nrhs), bf16(ni, nrhs), bf16(ni, nrhs),
        f32(exchanges, 4, face, nrhs), f32(ncon, ni), f32(4, ncon, face), bf16(256, ni), f32(256, ni), bf16(ni, 256),
        bf16(ncon, n_dev * ncon), bf16(ncon, n_dev * ncon),
        f32(256, 256), bf16(256, 256), bf16(256, 256),
        bf16(top_rows, 256), bf16(top_rows, 256), f32(256, top_pad), f32(top_pad, 256),
        f32(ncon, 128), f32(4, ncon, 128), f32(topc, n_group * topc), f32(2, topc, n_group * topc), f32(256, nrhs),
        f32(uses, 256, nrhs), f32(uses, 4, ncon, nrhs), f32(uses, n_dev, ncon, nrhs),
        f32(uses, n_dev, 2, per_dev, 128), f32(uses, n_dev, 2, per_dev, 128),
        f32(uses, n_group, 2, per_dev, 128), f32(uses, n_dev, 2, per_dev, 128),
        f32(uses, ncon, nrhs), f32(uses, 4, ncon, nrhs),
        f32(n_dev * ncon, nrhs), f32(per_dev, n_group * 64), f32(1, nrhs), f32(nrhs, nrhs), f32(1, nrhs),
        f32(uses, n_dev, 8, nrhs), f32(uses, n_group, 8, nrhs),
        f32(uses, n_dev, 8, nrhs), f32(uses, n_group, 8, nrhs),
        dma((4 + ni // 128,)), dma((3,)), dma((exchanges, 4)), dma((exchanges, 4)),
        dma((4,)), dma((4,)), dma((4,)), dma((4,)), dma((2,)), dma((2,)),
        dma((uses, 4)), dma((uses, 4)), dma((uses, 4)), dma((uses, 4)),
    ] + [dma((uses,))] * 16
    x, r, dirn, one = pl.pallas_call(
        functools.partial(main_kernel, n_group, n_dev),
        out_shape=[field] * 3 + [jax.ShapeDtypeStruct((1, nrhs), F32)],
        in_specs=[hbm, hbm, hbm, hbm, smem, vmem, vmem, vmem, vmem, vmem],
        out_specs=[hbm] * 3 + [vmem],
        scratch_shapes=scratch,
        compiler_params=pltpu.CompilerParams(
            collective_id=0, has_side_effects=True, vmem_limit_bytes=56 * 2**20
        ),
        cost_estimate=pl.CostEstimate(
            flops=18 * ni * ni * nrhs, bytes_accessed=4 * ni * ni + 24 * ni * nrhs, transcendentals=0
        ),
        name="pcg",
    )(
        applied_loads[0], stiffness[0], local_inverse[0], coarse_basis[0],
        face_index, face_index, coarse_map, group_inverse, top_basis, top_inverse,
    )
    return (x * one)[None], (r * one)[None], (dirn * one)[None]


def solution(mesh):
    both = ("group", "dev")
    return jax.shard_map(
        functools.partial(local, mesh.shape["group"], mesh.shape["dev"]),
        mesh=mesh,
        in_specs=(
            P(both, None, None), P(both, None, None), P(both, None, None), P(both, None, None),
            P(both, None), P(both, None), P(both, None), P(both, None), P("group", None),
        ),
        out_specs=(P(both, None, None),) * 3,
        check_vma=False,
    )
```

```python
import functools

import jax
import jax.numpy as jnp
from jax import lax
from jax.experimental import pallas as pl
from jax.experimental.pallas import tpu as pltpu
from jax.sharding import PartitionSpec as P

ITERS = 2
MESH = pl.DeviceIdType.MESH
F32 = jnp.float32
BF16 = jnp.bfloat16
NN = (((1,), (0,)), ((), ()))
NT = (((1,), (1,)), ((), ()))
CHUNK = 128
ROWS = 768


def dot(a, b, dims=NN):
    return lax.dot_general(a, b, dims, preferred_element_type=F32)


def split(a):
    hi = a.astype(BF16)
    return hi, (a - hi.astype(F32)).astype(BF16)


def dot3(a, b, dims=NN):
    (a_hi, a_lo), (b_hi, b_lo) = a, b
    return dot(a_hi, b_hi, dims) + (dot(a_lo, b_hi, dims) + dot(a_hi, b_lo, dims))


def fold(values):
    rows, cols = values.shape
    return jnp.sum(values.reshape(rows // 8, 8, cols), axis=0)


def main_kernel(
    n_group, n_dev,
    loads_hbm, stiff_hbm, inv_hbm, basis_hbm, pos_smem, cmap_row, ginv_ref, tbasis_ref, tinv_ref,
    x_out, r_out, d_out, one_out,
    loads, stiff, inv, basis, place_vec, place_smem,
    field, local_part, res, dirn, sol, prod, joined, weight, scaled, scaled_lo, plain,
    face_in, basis_f32, basis_in, basis_all, comb_t, comb,
    ginv_hi, ginv_lo, tb_all, tb_all_hi, tb_all_lo, t2_hi, t2_lo, tinv_all, turned,
    tb_own, tb_in, tinv_own, tinv_in, upper,
    parts, parts_in, coarse, u_out, u_in, top_in, ts_in, solved_own, solved_in,
    group_now, top_now, step_now, step_cols, norm_now, dot_dev, dot_group, curv_dev, curv_group,
    load_sem, out_sem, face_send, face_recv, basis_send, basis_recv, tb_send, tb_recv,
    tinv_send, tinv_recv, parts_send, parts_recv, solved_send, solved_recv,
    coarse_send, coarse_recv, u_send, u_recv, top_send, top_recv, ts_send, ts_recv,
    dd_send, dd_recv, dg_send, dg_recv, cd_send, cd_recv, cg_send, cg_recv,
):
    g = lax.axis_index("group")
    d = lax.axis_index("dev")
    ni, nrhs = loads.shape
    ncon = basis.shape[0]
    topc = tbasis_ref.shape[1]
    face = ni // 4
    per_dev = nrhs // n_dev
    has = [d > 0, d < n_dev - 1, g > 0, g < n_group - 1]
    target = [(g, d - 1), (g, d + 1), (g - 1, d), (g + 1, d)]
    opposite = [1, 0, 3, 2]
    w = [jnp.where(h, 0.5, 1.0).astype(F32) for h in has]

    def weight_of(b):
        return jnp.where(b == 0, w[0], jnp.where(b == 1, w[1], jnp.where(b == 2, w[2], w[3])))

    def dev_peer(i):
        return (g, lax.rem(d + i, n_dev))

    def group_peer(i):
        return (lax.rem(g + i, n_group), d)

    def fetch(src, dst, k):
        return pltpu.make_async_copy(src, dst, load_sem.at[k])

    fetch_loads = fetch(loads_hbm, loads, 0)
    fetch_basis = fetch(basis_hbm, basis, 1)
    fetch_inv = fetch(inv_hbm, inv, 2)
    fetch_stiff = fetch(stiff_hbm, stiff, 3)
    fetch_basis.start()
    fetch_loads.start()
    one_out[...] = jnp.ones_like(one_out)

    barrier = pltpu.get_barrier_semaphore()

    def greet_dev(i, carry):
        pl.semaphore_signal(barrier, inc=1, device_id=dev_peer(i), device_id_type=MESH)
        return carry

    def greet_group(i, carry):
        pl.semaphore_signal(barrier, inc=1, device_id=group_peer(i), device_id_type=MESH)
        return carry

    lax.fori_loop(1, n_dev, greet_dev, 0)
    lax.fori_loop(1, n_group, greet_group, 0)

    def spread(src_of, buf, k, send, recv, along_dev):
        n, me = (n_dev, d) if along_dev else (n_group, g)
        peer_of = dev_peer if along_dev else group_peer

        def body(i, carry):
            peer = peer_of(i)
            pltpu.make_async_remote_copy(
                src_ref=src_of(peer[1] if along_dev else peer[0]),
                dst_ref=buf.at[k, me],
                send_sem=send.at[k],
                recv_sem=recv.at[k],
                device_id=peer,
                device_id_type=MESH,
            ).start()
            return carry

        lax.fori_loop(1, n, body, 0)

    def all_of(buf, k, send, recv, along_dev):
        n = n_dev if along_dev else n_group
        part = buf.at[k, pl.ds(0, n - 1)]
        return pltpu.make_async_remote_copy(
            src_ref=part, dst_ref=part, send_sem=send.at[k], recv_sem=recv.at[k],
            device_id=dev_peer(1) if along_dev else group_peer(1), device_id_type=MESH,
        )

    def neighbour_copy(src, dst, send, recv, b):
        return pltpu.make_async_remote_copy(
            src_ref=src, dst_ref=dst, send_sem=send, recv_sem=recv,
            device_id=target[b], device_id_type=MESH,
        )

    def face_copy(src, e, b, slot):
        return neighbour_copy(
            src.at[pl.ds(b * face, face)], face_in.at[e, slot], face_send.at[e, b], face_recv.at[e, slot], b
        )

    def basis_copy(b, slot):
        return neighbour_copy(
            basis_f32.at[:, pl.ds(b * face, face)], basis_in.at[slot], basis_send.at[b], basis_recv.at[slot], b
        )

    def tb_copy(b, slot):
        return neighbour_copy(tb_own, tb_in.at[slot], tb_send.at[b], tb_recv.at[slot], b)

    def tinv_copy(b, slot):
        return neighbour_copy(tinv_own, tinv_in.at[slot - 2], tinv_send.at[b - 2], tinv_recv.at[slot - 2], b)

    def parts_copy(m, b, slot):
        return neighbour_copy(
            parts.at[m, pl.ds((b + 1) * ncon, ncon)], parts_in.at[m, slot],
            parts_send.at[m, b], parts_recv.at[m, slot], b,
        )

    def solved_copy(m, b, slot):
        return neighbour_copy(
            solved_own.at[m], solved_in.at[m, slot], solved_send.at[m, b], solved_recv.at[m, slot], b
        )

    def each_face(body, faces=(0, 1, 2, 3)):
        for b in faces:
            @pl.when(has[b])
            def _():
                body(b)

    def pick_rows(index, src, dst):
        def body(step, carry):
            base = step * 64
            for j in range(64):
                dst[pl.ds(base + j, 1), :] = src[pl.ds(index[0, base + j], 1), :]
            return carry

        lax.fori_loop(0, ni // 64, body, 0)

    def to_faces(src, dst):
        pick_rows(pos_smem, src, dst)

    def from_faces(src, dst):
        pick_rows(place_smem, src, dst)

    def over_chunks(body, init=0):
        per_face = face // CHUNK

        def step(i, carry):
            b = i // per_face
            at_in = pl.multiple_of((i - b * per_face) * CHUNK, CHUNK)
            return body(pl.ds(pl.multiple_of(i * CHUNK, CHUNK), CHUNK), b, pl.ds(at_in, CHUNK), carry)

        return lax.fori_loop(0, ni // CHUNK, step, init)

    def apply(matrix, vector, out, out_type):
        rows = ROWS if ni % ROWS == 0 else ni

        def body(i, carry):
            at = pl.ds(pl.multiple_of(i * rows, rows), rows)
            out[at, :] = dot(matrix[at, :], vector[...]).astype(out_type)
            return carry

        lax.fori_loop(0, ni // rows, body, 0)

    for b in range(4):
        @pl.when(jnp.logical_not(has[b]))
        def _():
            def zero_faces(e, carry):
                face_in[e, b] = jnp.zeros((face, nrhs), F32)
                return carry

            def zero_parts(m, carry):
                parts_in[m, b] = jnp.zeros((ncon, nrhs), F32)
                solved_in[m, b] = jnp.zeros((ncon, nrhs), F32)
                return carry

            lax.fori_loop(0, face_in.shape[0], zero_faces, 0)
            lax.fori_loop(0, ITERS + 1, zero_parts, 0)
            basis_in[b] = jnp.zeros((ncon, face), F32)
            tb_in[b] = jnp.zeros(tb_own.shape, F32)
            if b >= 2:
                tinv_in[b - 2] = jnp.zeros(tinv_own.shape, F32)

    spots = (
        lax.broadcasted_iota(jnp.int32, place_vec.shape, 0) * 128
        + lax.broadcasted_iota(jnp.int32, place_vec.shape, 1)
    )

    def invert(step, found):
        for j in range(64):
            k = step * 64 + j
            found = jnp.where(spots == pos_smem[0, k], k, found)
        return found

    place_vec[...] = lax.fori_loop(0, ni // 64, invert, jnp.zeros(place_vec.shape, jnp.int32))
    place_copies = [
        pltpu.make_async_copy(
            place_vec.at[pl.ds(i, 1)], place_smem.at[:, pl.ds(i * 128, 128)], load_sem.at[4 + i]
        )
        for i in range(ni // 128)
    ]
    for copy in place_copies:
        copy.start()

    select = jnp.where(
        lax.broadcasted_iota(jnp.int32, (ncon, ncon), 0) == cmap_row[...], 1.0, 0.0
    ).astype(BF16)
    fetch_basis.wait()
    fetch_loads.wait()
    fetch_inv.start()
    fetch_stiff.start()
    tb_own[...] = jnp.zeros_like(tb_own)
    tb_own[:, 0:topc] = tbasis_ref[...]
    tinv_own[...] = tinv_ref[...]

    def turn_basis(j, carry):
        at = pl.ds(pl.multiple_of(j * 128, 128), 128)
        block = dot(select, basis[:, at])
        prod[at, :] = jnp.concatenate([block, jnp.zeros((128 - ncon, 128), F32)], axis=0).T
        return carry

    lax.fori_loop(0, ni // 128, turn_basis, 0)
    to_faces(prod, local_part)

    def turn_back(j, carry):
        at = pl.ds(pl.multiple_of(j * 128, 128), 128)
        basis_f32[:, at] = local_part[at, :].T[0:ncon]
        return carry

    lax.fori_loop(0, ni // 128, turn_back, 0)
    pl.semaphore_wait(barrier, n_dev - 1 + n_group - 1)
    each_face(lambda b: basis_copy(b, opposite[b]).start())
    each_face(lambda b: tb_copy(b, opposite[b]).start())
    to_faces(loads, field)
    each_face(lambda b: face_copy(field, 0, b, opposite[b]).start())
    each_face(lambda b: tinv_copy(b, opposite[b]).start(), (2, 3))

    def clear(at, b, at_in, carry):
        zero = jnp.zeros((CHUNK, nrhs), F32)
        res[at, :] = zero
        dirn[at, :] = zero
        sol[at, :] = zero
        joined[at, :] = jnp.zeros((CHUNK, nrhs), F32) + weight_of(b)
        return carry

    over_chunks(clear)
    group_now[...] = jnp.zeros_like(group_now)
    top_now[...] = jnp.zeros_like(top_now)
    step_now[...] = jnp.full(step_now.shape, -1.0, F32)
    norm_now[...] = jnp.ones_like(norm_now)
    ginv_hi[...], ginv_lo[...] = split(ginv_ref[...])

    tb_all[...] = jnp.zeros_like(tb_all)
    each_face(lambda b: tb_copy(b, b).wait_recv())
    tb_all[0:ncon, 0:128] = tb_own[...]
    tb_all[ncon:2 * ncon, 0:128] = tb_in[0]
    tb_all[2 * ncon:3 * ncon, 0:128] = tb_in[1]
    tb_all[3 * ncon:4 * ncon, 128:256] = tb_in[2]
    tb_all[4 * ncon:5 * ncon, 128:256] = pltpu.roll(tb_in[3], 64, 1)
    tb_all[5 * ncon:5 * ncon + 8, 0:128] = jnp.where(
        (lax.broadcasted_iota(jnp.int32, (8, 128), 0) == 0)
        & (lax.broadcasted_iota(jnp.int32, (8, 128), 1) == 64), 1.0, 0.0,
    ).astype(F32)
    tb_all_hi[...], tb_all_lo[...] = split(tb_all[...])
    for copy in place_copies:
        copy.wait()
    from_faces(joined, weight)

    basis_all[...] = jnp.zeros_like(basis_all)
    basis_all[0:ncon, :] = basis_f32[...].astype(BF16)
    each_face(lambda b: basis_copy(b, b).wait_recv())
    for b in range(4):
        basis_all[(b + 1) * ncon:(b + 2) * ncon, b * face:(b + 1) * face] = basis_in[b].astype(BF16)

    def set_up_top():
        tinv_all[...] = jnp.zeros_like(tinv_all)
        cols = n_group * topc
        tinv_all[0:topc, 0:cols] = tinv_own[...]
        each_face(lambda b: tinv_copy(b, b).wait_recv(), (2, 3))
        tinv_all[128:128 + topc, 0:cols] = tinv_in[0]
        tinv_all[192:192 + topc, 0:cols] = tinv_in[1]

        def turn_over(j, carry):
            at = pl.ds(pl.multiple_of(j * 128, 128), 128)
            turned[at, :] = tinv_all[:, at].T
            return carry

        lax.fori_loop(0, turned.shape[0] // 128, turn_over, 0)
        t2_hi[...] = jnp.zeros_like(t2_hi)
        t2_lo[...] = jnp.zeros_like(t2_lo)

        def place(q, carry):
            hi, lo = split(turned[pl.ds(pl.multiple_of(q * topc, 16), topc), :])
            at = pl.ds(pl.multiple_of(q * 64, 64), topc)
            t2_hi[at, :] = hi
            t2_lo[at, :] = lo
            return carry

        lax.fori_loop(0, n_group, place, 0)

    def combine():
        for b in range(4):
            at = slice(b * face, (b + 1) * face)
            comb_t[0:ncon, at] = basis_f32[:, at]
            comb_t[ncon:2 * ncon, at] = basis_in[b]
            comb_t[2 * ncon:3 * ncon, at] = basis_f32[:, at]
            comb_t[3 * ncon:4 * ncon, at] = basis_in[b]
        comb_t[4 * ncon:, :] = jnp.zeros((256 - 4 * ncon, ni), F32)

        def turn_over(j, carry):
            at = pl.ds(pl.multiple_of(j * 128, 128), 128)
            comb[at, :] = comb_t[:, at].T.astype(BF16)
            return carry

        lax.fori_loop(0, ni // 128, turn_over, 0)

    odd = lax.rem(g, 2) == 1
    n_pairs = n_group // 2

    def total(buf, k):
        return jnp.sum(jnp.sum(buf[k], axis=0), axis=0, keepdims=True)

    def inner_of_plain():
        return over_chunks(
            lambda at, b, at_in, c: c + fold(plain[at, :].astype(F32) * prod[at, :]), jnp.zeros((8, nrhs), F32)
        )

    def iteration(it, carry):
        later = it > 0

        @pl.when(later)
        def _():
            @pl.when(it == 1)
            def _():
                fetch_stiff.wait()

            apply(stiff, plain, prod, F32)
            curv_dev[it, d] = inner_of_plain()
            spread(lambda p: curv_dev.at[it, d], curv_dev, it, cd_send, cd_recv, True)
            to_faces(prod, field)

        def halves(at, b, at_in, c):
            hi, lo = split(weight_of(b) * field[at, :])
            scaled[at, :] = hi
            scaled_lo[at, :] = lo
            return c

        over_chunks(halves)
        shares = dot(basis_all[...], scaled[...]) + dot(basis_all[...], scaled_lo[...])
        parts[it] = shares
        u_t = dot3(split(shares.T), (tb_all_hi[...], tb_all_lo[...]))
        u_out[it, :, 0] = u_t[:, 0:128].reshape(n_dev, per_dev, 128)
        u_out[it, :, 1] = u_t[:, 128:256].reshape(n_dev, per_dev, 128)
        u_in[it, d] = u_out[it, d]
        spread(lambda p: u_out.at[it, p], u_in, it, u_send, u_recv, True)
        each_face(lambda b: parts_copy(it, b, opposite[b]).start())

        @pl.when(later)
        def _():
            each_face(lambda b: face_copy(field, 2 * it, b, opposite[b]).start())

        @pl.when(it == 0)
        def _():
            set_up_top()

        each_face(lambda b: parts_copy(it, b, b).wait_recv())
        own_coarse = parts[it, 0:ncon] + (
            (parts_in[it, 0] + parts_in[it, 1]) + (parts_in[it, 2] + parts_in[it, 3])
        )
        coarse[it, d] = own_coarse
        spread(lambda p: coarse.at[it, d], coarse, it, coarse_send, coarse_recv, True)

        @pl.when(later)
        def _():
            all_of(curv_dev, it, cd_send, cd_recv, True).wait_recv()
            curv_group[it, g] = jnp.sum(curv_dev[it], axis=0)
            spread(lambda p: curv_group.at[it, g], curv_group, it, cg_send, cg_recv, False)

        all_of(u_in, it, u_send, u_recv, True).wait_recv()
        own_tile = jnp.sum(u_in[it, :, 0], axis=0)
        side_tile = jnp.sum(u_in[it, :, 1], axis=0)
        lane = lax.broadcasted_iota(jnp.int32, own_tile.shape, 1)
        keep = jnp.where(odd, lane, 127 - lane) < 64
        top_in[it, g, 0] = jnp.where(odd, pltpu.roll(own_tile, 64, 1), own_tile) + jnp.where(
            keep, side_tile, 0.0
        )
        top_in[it, g, 1] = pltpu.roll(jnp.where(keep, 0.0, side_tile), 64, 1)
        spread(lambda p: top_in.at[it, g], top_in, it, top_send, top_recv, False)

        @pl.when(it == 0)
        def _():
            combine()

        each_face(lambda b: face_copy(field, 2 * it, b, b).wait_recv())

        def assemble(at, b, at_in, c):
            joined[at, :] = field[at, :] + face_in[2 * it, b, at_in, :]
            return c

        over_chunks(assemble)
        from_faces(joined, prod)

        @pl.when(later)
        def _():
            @pl.when(it == 1)
            def _():
                all_of(dot_group, 0, dg_send, dg_recv, False).wait_recv()
                norm_now[...] = total(dot_group, 0)

            all_of(curv_group, it, cg_send, cg_recv, False).wait_recv()
            step_now[...] = norm_now[...] / total(curv_group, it)

        step_size = step_now[...]
        step_cols[...] = jnp.broadcast_to(step_size, step_cols.shape).T
        step_col = step_cols[pl.ds(pl.multiple_of(d * per_dev, per_dev), per_dev), :]

        def update(at, b, at_in, c):
            value = res[at, :] - step_size * prod[at, :]
            res[at, :] = value
            plain[at, :] = (weight[at, :] * value).astype(BF16)
            return c

        over_chunks(update)

        @pl.when(it == 0)
        def _():
            fetch_inv.wait()

        apply(inv, plain, prod, F32)

        all_of(top_in, it, top_send, top_recv, False).wait_recv()
        every = top_in[it]
        pairs = []
        for p in range(n_pairs):
            pair = every[2 * p, 0] + every[2 * p + 1, 0]
            if p > 0:
                pair = pair + every[2 * p - 1, 1]
            if p < n_pairs - 1:
                pair = pair + every[2 * p + 2, 1]
            pairs.append(top_now[:, p * 128:(p + 1) * 128] - step_col * pair)
        top_next = jnp.concatenate(pairs, axis=1)
        top_now[...] = top_next
        ts = dot3(split(top_next), (t2_hi[...], t2_lo[...]))
        own_pair = top_now[:, pl.ds(pl.multiple_of(g // 2 * 128, 128), 128)]
        own_top = jnp.where(odd, pltpu.roll(own_pair, 64, 1), own_pair)
        top_energy = jnp.sum(jnp.where(lane < topc, ts[:, 0:128] * own_top, 0.0), axis=1, keepdims=True)
        ts_in[it, d, 0] = jnp.where(lane == 64, top_energy, ts[:, 0:128])
        ts_in[it, d, 1] = ts[:, 128:256]
        spread(lambda p: ts_in.at[it, d], ts_in, it, ts_send, ts_recv, True)

        all_of(coarse, it, coarse_send, coarse_recv, True).wait_recv()
        group_next = group_now[...] - step_size * coarse[it].reshape(n_dev * ncon, nrhs)
        group_now[...] = group_next
        solved = dot3((ginv_hi[...], ginv_lo[...]), split(group_next))
        solved_own[it] = solved
        each_face(lambda b: solved_copy(it, b, opposite[b]).start())

        energy = inner_of_plain()
        own_coarse_now = group_now[pl.ds(pl.multiple_of(d * ncon, 16), ncon), :]
        dot_dev[it, d] = energy + fold(own_coarse_now * solved)
        spread(lambda p: dot_dev.at[it, d], dot_dev, it, dd_send, dd_recv, True)
        to_faces(prod, local_part)
        each_face(lambda b: face_copy(local_part, 2 * it + 1, b, opposite[b]).start())

        def advance(at, b, at_in, c):
            sol[at, :] = sol[at, :] + step_size * dirn[at, :]
            return c

        over_chunks(advance)

        @pl.when(it == ITERS)
        def _():
            pltpu.make_async_copy(sol, x_out, out_sem.at[0]).start()
            pltpu.make_async_copy(res, r_out, out_sem.at[1]).start()

        all_of(ts_in, it, ts_send, ts_recv, True).wait_recv()
        ts_all = jnp.concatenate(
            [ts_in[it, :, 0].reshape(nrhs, 128), ts_in[it, :, 1].reshape(nrhs, 128)], axis=1
        )
        upper[...] = dot3((tb_all_hi[...], tb_all_lo[...]), split(ts_all), NT)

        all_of(dot_dev, it, dd_send, dd_recv, True).wait_recv()
        line = lax.broadcasted_iota(jnp.int32, (8, nrhs), 0)
        dot_group[it, g] = jnp.sum(dot_dev[it], axis=0) + jnp.where(
            line == 0, upper[5 * ncon:5 * ncon + 1, :], 0.0
        )
        spread(lambda p: dot_group.at[it, g], dot_group, it, dg_send, dg_recv, False)

        own_hi, own_lo = split(solved + upper[0:ncon, :])
        each_face(lambda b: solved_copy(it, b, b).wait_recv())
        each_face(lambda b: face_copy(local_part, 2 * it + 1, b, b).wait_recv())

        def join(b, c):
            above = upper[pl.ds(pl.multiple_of((b + 1) * ncon, 16), ncon), :]
            in_hi, in_lo = split(solved_in[it, b] + above)
            values = jnp.concatenate(
                [own_hi, in_hi, own_lo, in_lo, jnp.zeros((256 - 4 * ncon, nrhs), BF16)], axis=0
            )
            at = pl.ds(pl.multiple_of(b * face, face), face)
            joined[at, :] = weight_of(b) * (
                local_part[at, :] + face_in[2 * it + 1, b] + dot(comb[at, :], values)
            )
            return c

        lax.fori_loop(0, 4, join, 0)
        from_faces(joined, prod)

        all_of(u_in, it, u_send, u_recv, True).wait_send()
        all_of(coarse, it, coarse_send, coarse_recv, True).wait_send()
        all_of(top_in, it, top_send, top_recv, False).wait_send()
        all_of(ts_in, it, ts_send, ts_recv, True).wait_send()
        all_of(dot_dev, it, dd_send, dd_recv, True).wait_send()

        def left(b):
            face_copy(field, 2 * it, b, opposite[b]).wait_send()
            face_copy(local_part, 2 * it + 1, b, opposite[b]).wait_send()
            parts_copy(it, b, opposite[b]).wait_send()
            solved_copy(it, b, opposite[b]).wait_send()

        each_face(left)

        @pl.when(later)
        def _():
            all_of(curv_dev, it, cd_send, cd_recv, True).wait_send()
            all_of(curv_group, it, cg_send, cg_recv, False).wait_send()
            all_of(dot_group, it, dg_send, dg_recv, False).wait_recv()
            norm_next = total(dot_group, it)
            step_now[...] = norm_next / norm_now[...]
            norm_now[...] = norm_next

        ratio = step_now[...]

        def turn(at, b, at_in, c):
            value = prod[at, :] + ratio * dirn[at, :]
            dirn[at, :] = value
            plain[at, :] = value.astype(BF16)
            return c

        over_chunks(turn)
        return carry

    lax.fori_loop(0, ITERS + 1, iteration, 0)

    store = pltpu.make_async_copy(dirn, d_out, out_sem.at[2])
    store.start()
    for m in range(ITERS + 1):
        all_of(dot_group, m, dg_send, dg_recv, False).wait_send()
    each_face(lambda b: basis_copy(b, opposite[b]).wait_send())
    each_face(lambda b: tb_copy(b, opposite[b]).wait_send())
    each_face(lambda b: tinv_copy(b, opposite[b]).wait_send(), (2, 3))
    pltpu.make_async_copy(sol, x_out, out_sem.at[0]).wait()
    pltpu.make_async_copy(res, r_out, out_sem.at[1]).wait()
    store.wait()


def local(
    n_group, n_dev,
    applied_loads, stiffness, local_inverse, coarse_basis, face_index, coarse_map, group_inverse, top_basis, top_inverse,
):
    ni, nrhs = applied_loads.shape[1:]
    ncon = coarse_basis.shape[1]
    topc = top_basis.shape[1]
    face = ni // 4
    per_dev = nrhs // n_dev
    uses = ITERS + 1
    exchanges = 2 * uses
    top_rows = n_group * 64
    top_pad = (n_group * topc + 127) // 128 * 128
    vmem = pl.BlockSpec(memory_space=pltpu.VMEM)
    smem = pl.BlockSpec(memory_space=pltpu.SMEM)
    hbm = pl.BlockSpec(memory_space=pl.ANY)
    field = jax.ShapeDtypeStruct((ni, nrhs), F32)
    dma = pltpu.SemaphoreType.DMA

    def f32(*shape):
        return pltpu.VMEM(shape, F32)

    def bf16(*shape):
        return pltpu.VMEM(shape, BF16)

    scratch = [
        f32(ni, nrhs), bf16(ni, ni), bf16(ni, ni), bf16(ncon, ni),
        pltpu.VMEM((ni // 128, 128), jnp.int32), pltpu.SMEM((1, ni), jnp.int32),
        f32(ni, nrhs),
        f32(ni, nrhs), f32(ni, nrhs), f32(ni, nrhs), f32(ni, nrhs), f32(ni, nrhs), f32(ni, nrhs), f32(ni, nrhs),
        bf16(ni, nrhs), bf16(ni, nrhs), bf16(ni, nrhs),
        f32(exchanges, 4, face, nrhs), f32(ncon, ni), f32(4, ncon, face), bf16(256, ni), f32(256, ni), bf16(ni, 256),
        bf16(ncon, n_dev * ncon), bf16(ncon, n_dev * ncon),
        f32(256, 256), bf16(256, 256), bf16(256, 256),
        bf16(top_rows, 256), bf16(top_rows, 256), f32(256, top_pad), f32(top_pad, 256),
        f32(ncon, 128), f32(4, ncon, 128), f32(topc, n_group * topc), f32(2, topc, n_group * topc), f32(256, nrhs),
        f32(uses, 256, nrhs), f32(uses, 4, ncon, nrhs), f32(uses, n_dev, ncon, nrhs),
        f32(uses, n_dev, 2, per_dev, 128), f32(uses, n_dev, 2, per_dev, 128),
        f32(uses, n_group, 2, per_dev, 128), f32(uses, n_dev, 2, per_dev, 128),
        f32(uses, ncon, nrhs), f32(uses, 4, ncon, nrhs),
        f32(n_dev * ncon, nrhs), f32(per_dev, n_group * 64), f32(1, nrhs), f32(nrhs, nrhs), f32(1, nrhs),
        f32(uses, n_dev, 8, nrhs), f32(uses, n_group, 8, nrhs),
        f32(uses, n_dev, 8, nrhs), f32(uses, n_group, 8, nrhs),
        dma((4 + ni // 128,)), dma((3,)), dma((exchanges, 4)), dma((exchanges, 4)),
        dma((4,)), dma((4,)), dma((4,)), dma((4,)), dma((2,)), dma((2,)),
        dma((uses, 4)), dma((uses, 4)), dma((uses, 4)), dma((uses, 4)),
    ] + [dma((uses,))] * 16
    x, r, dirn, one = pl.pallas_call(
        functools.partial(main_kernel, n_group, n_dev),
        out_shape=[field] * 3 + [jax.ShapeDtypeStruct((1, nrhs), F32)],
        in_specs=[hbm, hbm, hbm, hbm, smem, vmem, vmem, vmem, vmem],
        out_specs=[hbm] * 3 + [vmem],
        scratch_shapes=scratch,
        compiler_params=pltpu.CompilerParams(
            collective_id=0, has_side_effects=True, vmem_limit_bytes=56 * 2**20
        ),
        cost_estimate=pl.CostEstimate(
            flops=18 * ni * ni * nrhs, bytes_accessed=4 * ni * ni + 24 * ni * nrhs, transcendentals=0
        ),
        name="pcg",
    )(
        applied_loads[0], stiffness[0], local_inverse[0], coarse_basis[0],
        face_index, coarse_map, group_inverse, top_basis, top_inverse,
    )
    return (x * one)[None], (r * one)[None], (dirn * one)[None]


def solution(mesh):
    both = ("group", "dev")
    return jax.shard_map(
        functools.partial(local, mesh.shape["group"], mesh.shape["dev"]),
        mesh=mesh,
        in_specs=(
            P(both, None, None), P(both, None, None), P(both, None, None), P(both, None, None),
            P(both, None), P(both, None), P(both, None), P(both, None), P("group", None),
        ),
        out_specs=(P(both, None, None),) * 3,
        check_vma=False,
    )
```

```python
import functools

import jax
import jax.numpy as jnp
from jax import lax
from jax.experimental import pallas as pl
from jax.experimental.pallas import tpu as pltpu
from jax.sharding import PartitionSpec as P

ITERS = 2
MESH = pl.DeviceIdType.MESH
F32 = jnp.float32
BF16 = jnp.bfloat16
NN = (((1,), (0,)), ((), ()))
NT = (((1,), (1,)), ((), ()))
CHUNK = 128
ROWS = 768


def dot(a, b, dims=NN):
    return lax.dot_general(a, b, dims, preferred_element_type=F32)


def split(a):
    hi = a.astype(BF16)
    return hi, (a - hi.astype(F32)).astype(BF16)


def dot3(a, b, dims=NN):
    (a_hi, a_lo), (b_hi, b_lo) = a, b
    return dot(a_hi, b_hi, dims) + (dot(a_lo, b_hi, dims) + dot(a_hi, b_lo, dims))


def fold(values):
    rows, cols = values.shape
    return jnp.sum(values.reshape(rows // 8, 8, cols), axis=0)


def main_kernel(
    n_group, n_dev,
    loads_hbm, stiff_hbm, inv_hbm, basis_hbm, pos_smem, cmap_row, ginv_ref, tbasis_ref, tinv_ref,
    x_out, r_out, d_out, one_out,
    loads, stiff, inv, basis, place_vec, place_smem,
    field, local_part, res, dirn, sol, prod, joined, weight, scaled, scaled_lo, plain,
    face_in, basis_f32, basis_in, basis_all, comb_t, comb,
    ginv_hi, ginv_lo, tb_all, tb_all_hi, tb_all_lo, t2_hi, t2_lo, tinv_all, turned,
    tb_own, tb_in, tinv_own, tinv_in, upper,
    parts, parts_in, coarse, u_out, u_in, top_in, ts_in, solved_own, solved_in,
    group_now, top_now, step_now, step_cols, norm_now, dot_dev, dot_group, curv_dev, curv_group,
    load_sem, out_sem, face_send, face_recv, basis_send, basis_recv, tb_send, tb_recv,
    tinv_send, tinv_recv, parts_send, parts_recv, solved_send, solved_recv,
    coarse_send, coarse_recv, u_send, u_recv, top_send, top_recv, ts_send, ts_recv,
    dd_send, dd_recv, dg_send, dg_recv, cd_send, cd_recv, cg_send, cg_recv,
):
    g = lax.axis_index("group")
    d = lax.axis_index("dev")
    ni, nrhs = loads.shape
    ncon = basis.shape[0]
    topc = tbasis_ref.shape[1]
    face = ni // 4
    per_dev = nrhs // n_dev
    has = [d > 0, d < n_dev - 1, g > 0, g < n_group - 1]
    target = [(g, d - 1), (g, d + 1), (g - 1, d), (g + 1, d)]
    opposite = [1, 0, 3, 2]
    w = [jnp.where(h, 0.5, 1.0).astype(F32) for h in has]

    def weight_of(b):
        return jnp.where(b == 0, w[0], jnp.where(b == 1, w[1], jnp.where(b == 2, w[2], w[3])))

    def dev_peer(i):
        return (g, lax.rem(d + i, n_dev))

    def group_peer(i):
        return (lax.rem(g + i, n_group), d)

    def fetch(src, dst, k):
        return pltpu.make_async_copy(src, dst, load_sem.at[k])

    fetch_loads = fetch(loads_hbm, loads, 0)
    fetch_basis = fetch(basis_hbm, basis, 1)
    fetch_inv = fetch(inv_hbm, inv, 2)
    fetch_stiff = fetch(stiff_hbm, stiff, 3)
    fetch_basis.start()
    fetch_loads.start()
    one_out[...] = jnp.ones_like(one_out)

    barrier = pltpu.get_barrier_semaphore()

    def greet_dev(i, carry):
        pl.semaphore_signal(barrier, inc=1, device_id=dev_peer(i), device_id_type=MESH)
        return carry

    def greet_group(i, carry):
        pl.semaphore_signal(barrier, inc=1, device_id=group_peer(i), device_id_type=MESH)
        return carry

    lax.fori_loop(1, n_dev, greet_dev, 0)
    lax.fori_loop(1, n_group, greet_group, 0)

    def spread(src_of, buf, k, send, recv, along_dev):
        n, me = (n_dev, d) if along_dev else (n_group, g)
        peer_of = dev_peer if along_dev else group_peer

        def body(i, carry):
            peer = peer_of(i)
            pltpu.make_async_remote_copy(
                src_ref=src_of(peer[1] if along_dev else peer[0]),
                dst_ref=buf.at[k, me],
                send_sem=send.at[k],
                recv_sem=recv.at[k],
                device_id=peer,
                device_id_type=MESH,
            ).start()
            return carry

        lax.fori_loop(1, n, body, 0, unroll=5)

    def all_of(buf, k, send, recv, along_dev):
        n = n_dev if along_dev else n_group
        part = buf.at[k, pl.ds(0, n - 1)]
        return pltpu.make_async_remote_copy(
            src_ref=part, dst_ref=part, send_sem=send.at[k], recv_sem=recv.at[k],
            device_id=dev_peer(1) if along_dev else group_peer(1), device_id_type=MESH,
        )

    def neighbour_copy(src, dst, send, recv, b):
        return pltpu.make_async_remote_copy(
            src_ref=src, dst_ref=dst, send_sem=send, recv_sem=recv,
            device_id=target[b], device_id_type=MESH,
        )

    def face_copy(src, e, b, slot):
        return neighbour_copy(
            src.at[pl.ds(b * face, face)], face_in.at[e, slot], face_send.at[e, b], face_recv.at[e, slot], b
        )

    def basis_copy(b, slot):
        return neighbour_copy(
            basis_f32.at[:, pl.ds(b * face, face)], basis_in.at[slot], basis_send.at[b], basis_recv.at[slot], b
        )

    def tb_copy(b, slot):
        return neighbour_copy(tb_own, tb_in.at[slot], tb_send.at[b], tb_recv.at[slot], b)

    def tinv_copy(b, slot):
        return neighbour_copy(tinv_own, tinv_in.at[slot - 2], tinv_send.at[b - 2], tinv_recv.at[slot - 2], b)

    def parts_copy(m, b, slot):
        return neighbour_copy(
            parts.at[m, pl.ds((b + 1) * ncon, ncon)], parts_in.at[m, slot],
            parts_send.at[m, b], parts_recv.at[m, slot], b,
        )

    def solved_copy(m, b, slot):
        return neighbour_copy(
            solved_own.at[m], solved_in.at[m, slot], solved_send.at[m, b], solved_recv.at[m, slot], b
        )

    def each_face(body, faces=(0, 1, 2, 3)):
        for b in faces:
            @pl.when(has[b])
            def _():
                body(b)

    def pick_rows(index, src, dst):
        def body(step, carry):
            base = step * 128
            for j in range(128):
                dst[pl.ds(base + j, 1), :] = src[pl.ds(index[0, base + j], 1), :]
            return carry

        lax.fori_loop(0, ni // 128, body, 0)

    def to_faces(src, dst):
        pick_rows(pos_smem, src, dst)

    def from_faces(src, dst):
        pick_rows(place_smem, src, dst)

    def over_chunks(body, init=0):
        per_face = face // CHUNK

        def step(i, carry):
            b = i // per_face
            at_in = pl.multiple_of((i - b * per_face) * CHUNK, CHUNK)
            return body(pl.ds(pl.multiple_of(i * CHUNK, CHUNK), CHUNK), b, pl.ds(at_in, CHUNK), carry)

        return lax.fori_loop(0, ni // CHUNK, step, init)

    def apply(matrix, vector, out, out_type):
        rows = ROWS if ni % ROWS == 0 else ni

        def body(i, carry):
            at = pl.ds(pl.multiple_of(i * rows, rows), rows)
            out[at, :] = dot(matrix[at, :], vector[...]).astype(out_type)
            return carry

        lax.fori_loop(0, ni // rows, body, 0)

    for b in range(4):
        @pl.when(jnp.logical_not(has[b]))
        def _():
            def zero_faces(e, carry):
                face_in[e, b] = jnp.zeros((face, nrhs), F32)
                return carry

            def zero_parts(m, carry):
                parts_in[m, b] = jnp.zeros((ncon, nrhs), F32)
                solved_in[m, b] = jnp.zeros((ncon, nrhs), F32)
                return carry

            lax.fori_loop(0, face_in.shape[0], zero_faces, 0)
            lax.fori_loop(0, ITERS + 1, zero_parts, 0)
            basis_in[b] = jnp.zeros((ncon, face), F32)
            tb_in[b] = jnp.zeros(tb_own.shape, F32)
            if b >= 2:
                tinv_in[b - 2] = jnp.zeros(tinv_own.shape, F32)

    spots = (
        lax.broadcasted_iota(jnp.int32, place_vec.shape, 0) * 128
        + lax.broadcasted_iota(jnp.int32, place_vec.shape, 1)
    )

    def invert(step, found):
        for j in range(128):
            k = step * 128 + j
            found = jnp.where(spots == pos_smem[0, k], k, found)
        return found

    place_vec[...] = lax.fori_loop(0, ni // 128, invert, jnp.zeros(place_vec.shape, jnp.int32))
    place_copies = [
        pltpu.make_async_copy(
            place_vec.at[pl.ds(i, 1)], place_smem.at[:, pl.ds(i * 128, 128)], load_sem.at[4 + i]
        )
        for i in range(ni // 128)
    ]
    for copy in place_copies:
        copy.start()

    select = jnp.where(
        lax.broadcasted_iota(jnp.int32, (ncon, ncon), 0) == cmap_row[...], 1.0, 0.0
    ).astype(BF16)
    fetch_basis.wait()
    fetch_loads.wait()
    fetch_inv.start()
    fetch_stiff.start()
    tb_own[...] = jnp.zeros_like(tb_own)
    tb_own[:, 0:topc] = tbasis_ref[...]
    tinv_own[...] = tinv_ref[...]

    def turn_basis(j, carry):
        at = pl.ds(pl.multiple_of(j * 128, 128), 128)
        block = dot(select, basis[:, at])
        prod[at, :] = jnp.concatenate([block, jnp.zeros((128 - ncon, 128), F32)], axis=0).T
        return carry

    lax.fori_loop(0, ni // 128, turn_basis, 0)
    to_faces(prod, local_part)

    def turn_back(j, carry):
        at = pl.ds(pl.multiple_of(j * 128, 128), 128)
        basis_f32[:, at] = local_part[at, :].T[0:ncon]
        return carry

    lax.fori_loop(0, ni // 128, turn_back, 0)
    pl.semaphore_wait(barrier, n_dev - 1 + n_group - 1)
    each_face(lambda b: basis_copy(b, opposite[b]).start())
    each_face(lambda b: tb_copy(b, opposite[b]).start())
    to_faces(loads, field)
    each_face(lambda b: face_copy(field, 0, b, opposite[b]).start())
    each_face(lambda b: tinv_copy(b, opposite[b]).start(), (2, 3))

    def clear(at, b, at_in, carry):
        zero = jnp.zeros((CHUNK, nrhs), F32)
        res[at, :] = zero
        dirn[at, :] = zero
        sol[at, :] = zero
        joined[at, :] = jnp.zeros((CHUNK, nrhs), F32) + weight_of(b)
        return carry

    over_chunks(clear)
    group_now[...] = jnp.zeros_like(group_now)
    top_now[...] = jnp.zeros_like(top_now)
    step_now[...] = jnp.full(step_now.shape, -1.0, F32)
    norm_now[...] = jnp.ones_like(norm_now)
    ginv_hi[...], ginv_lo[...] = split(ginv_ref[...])

    tb_all[...] = jnp.zeros_like(tb_all)
    each_face(lambda b: tb_copy(b, b).wait_recv())
    tb_all[0:ncon, 0:128] = tb_own[...]
    tb_all[ncon:2 * ncon, 0:128] = tb_in[0]
    tb_all[2 * ncon:3 * ncon, 0:128] = tb_in[1]
    tb_all[3 * ncon:4 * ncon, 128:256] = tb_in[2]
    tb_all[4 * ncon:5 * ncon, 128:256] = pltpu.roll(tb_in[3], 64, 1)
    tb_all[5 * ncon:5 * ncon + 8, 0:128] = jnp.where(
        (lax.broadcasted_iota(jnp.int32, (8, 128), 0) == 0)
        & (lax.broadcasted_iota(jnp.int32, (8, 128), 1) == 64), 1.0, 0.0,
    ).astype(F32)
    tb_all_hi[...], tb_all_lo[...] = split(tb_all[...])
    for copy in place_copies:
        copy.wait()
    from_faces(joined, weight)

    basis_all[...] = jnp.zeros_like(basis_all)
    basis_all[0:ncon, :] = basis_f32[...].astype(BF16)
    each_face(lambda b: basis_copy(b, b).wait_recv())
    for b in range(4):
        basis_all[(b + 1) * ncon:(b + 2) * ncon, b * face:(b + 1) * face] = basis_in[b].astype(BF16)

    def set_up_top():
        tinv_all[...] = jnp.zeros_like(tinv_all)
        cols = n_group * topc
        tinv_all[0:topc, 0:cols] = tinv_own[...]
        each_face(lambda b: tinv_copy(b, b).wait_recv(), (2, 3))
        tinv_all[128:128 + topc, 0:cols] = tinv_in[0]
        tinv_all[192:192 + topc, 0:cols] = tinv_in[1]

        def turn_over(j, carry):
            at = pl.ds(pl.multiple_of(j * 128, 128), 128)
            turned[at, :] = tinv_all[:, at].T
            return carry

        lax.fori_loop(0, turned.shape[0] // 128, turn_over, 0)
        t2_hi[...] = jnp.zeros_like(t2_hi)
        t2_lo[...] = jnp.zeros_like(t2_lo)

        def place(q, carry):
            hi, lo = split(turned[pl.ds(pl.multiple_of(q * topc, 16), topc), :])
            at = pl.ds(pl.multiple_of(q * 64, 64), topc)
            t2_hi[at, :] = hi
            t2_lo[at, :] = lo
            return carry

        lax.fori_loop(0, n_group, place, 0)

    def combine():
        for b in range(4):
            at = slice(b * face, (b + 1) * face)
            comb_t[0:ncon, at] = basis_f32[:, at]
            comb_t[ncon:2 * ncon, at] = basis_in[b]
            comb_t[2 * ncon:3 * ncon, at] = basis_f32[:, at]
            comb_t[3 * ncon:4 * ncon, at] = basis_in[b]
        comb_t[4 * ncon:, :] = jnp.zeros((256 - 4 * ncon, ni), F32)

        def turn_over(j, carry):
            at = pl.ds(pl.multiple_of(j * 128, 128), 128)
            comb[at, :] = comb_t[:, at].T.astype(BF16)
            return carry

        lax.fori_loop(0, ni // 128, turn_over, 0)

    odd = lax.rem(g, 2) == 1
    n_pairs = n_group // 2

    def total(buf, k):
        return jnp.sum(jnp.sum(buf[k], axis=0), axis=0, keepdims=True)

    def inner_of_plain():
        return over_chunks(
            lambda at, b, at_in, c: c + fold(plain[at, :].astype(F32) * prod[at, :]), jnp.zeros((8, nrhs), F32)
        )

    def iteration(it, carry):
        later = it > 0

        @pl.when(later)
        def _():
            @pl.when(it == 1)
            def _():
                fetch_stiff.wait()

            apply(stiff, plain, prod, F32)
            curv_dev[it, d] = inner_of_plain()
            spread(lambda p: curv_dev.at[it, d], curv_dev, it, cd_send, cd_recv, True)
            to_faces(prod, field)

        def halves(at, b, at_in, c):
            hi, lo = split(weight_of(b) * field[at, :])
            scaled[at, :] = hi
            scaled_lo[at, :] = lo
            return c

        over_chunks(halves)
        shares = dot(basis_all[...], scaled[...]) + dot(basis_all[...], scaled_lo[...])
        parts[it] = shares
        u_t = dot3(split(shares.T), (tb_all_hi[...], tb_all_lo[...]))
        u_out[it, :, 0] = u_t[:, 0:128].reshape(n_dev, per_dev, 128)
        u_out[it, :, 1] = u_t[:, 128:256].reshape(n_dev, per_dev, 128)
        u_in[it, d] = u_out[it, d]
        spread(lambda p: u_out.at[it, p], u_in, it, u_send, u_recv, True)
        each_face(lambda b: parts_copy(it, b, opposite[b]).start())

        @pl.when(later)
        def _():
            each_face(lambda b: face_copy(field, 2 * it, b, opposite[b]).start())

        @pl.when(it == 0)
        def _():
            set_up_top()

        each_face(lambda b: parts_copy(it, b, b).wait_recv())
        own_coarse = parts[it, 0:ncon] + (
            (parts_in[it, 0] + parts_in[it, 1]) + (parts_in[it, 2] + parts_in[it, 3])
        )
        coarse[it, d] = own_coarse
        spread(lambda p: coarse.at[it, d], coarse, it, coarse_send, coarse_recv, True)

        @pl.when(later)
        def _():
            all_of(curv_dev, it, cd_send, cd_recv, True).wait_recv()
            curv_group[it, g] = jnp.sum(curv_dev[it], axis=0)
            spread(lambda p: curv_group.at[it, g], curv_group, it, cg_send, cg_recv, False)

        all_of(u_in, it, u_send, u_recv, True).wait_recv()
        own_tile = jnp.sum(u_in[it, :, 0], axis=0)
        side_tile = jnp.sum(u_in[it, :, 1], axis=0)
        lane = lax.broadcasted_iota(jnp.int32, own_tile.shape, 1)
        keep = jnp.where(odd, lane, 127 - lane) < 64
        top_in[it, g, 0] = jnp.where(odd, pltpu.roll(own_tile, 64, 1), own_tile) + jnp.where(
            keep, side_tile, 0.0
        )
        top_in[it, g, 1] = pltpu.roll(jnp.where(keep, 0.0, side_tile), 64, 1)
        spread(lambda p: top_in.at[it, g], top_in, it, top_send, top_recv, False)

        @pl.when(it == 0)
        def _():
            combine()

        each_face(lambda b: face_copy(field, 2 * it, b, b).wait_recv())

        def assemble(at, b, at_in, c):
            joined[at, :] = field[at, :] + face_in[2 * it, b, at_in, :]
            return c

        over_chunks(assemble)
        from_faces(joined, prod)

        @pl.when(later)
        def _():
            @pl.when(it == 1)
            def _():
                all_of(dot_group, 0, dg_send, dg_recv, False).wait_recv()
                norm_now[...] = total(dot_group, 0)

            all_of(curv_group, it, cg_send, cg_recv, False).wait_recv()
            step_now[...] = norm_now[...] / total(curv_group, it)

        step_size = step_now[...]
        step_cols[...] = jnp.broadcast_to(step_size, step_cols.shape).T
        step_col = step_cols[pl.ds(pl.multiple_of(d * per_dev, per_dev), per_dev), :]

        def update(at, b, at_in, c):
            value = res[at, :] - step_size * prod[at, :]
            res[at, :] = value
            plain[at, :] = (weight[at, :] * value).astype(BF16)
            return c

        over_chunks(update)

        @pl.when(it == 0)
        def _():
            fetch_inv.wait()

        apply(inv, plain, prod, F32)

        all_of(top_in, it, top_send, top_recv, False).wait_recv()
        every = top_in[it]
        pairs = []
        for p in range(n_pairs):
            pair = every[2 * p, 0] + every[2 * p + 1, 0]
            if p > 0:
                pair = pair + every[2 * p - 1, 1]
            if p < n_pairs - 1:
                pair = pair + every[2 * p + 2, 1]
            pairs.append(top_now[:, p * 128:(p + 1) * 128] - step_col * pair)
        top_next = jnp.concatenate(pairs, axis=1)
        top_now[...] = top_next
        ts = dot3(split(top_next), (t2_hi[...], t2_lo[...]))
        own_pair = top_now[:, pl.ds(pl.multiple_of(g // 2 * 128, 128), 128)]
        own_top = jnp.where(odd, pltpu.roll(own_pair, 64, 1), own_pair)
        top_energy = jnp.sum(jnp.where(lane < topc, ts[:, 0:128] * own_top, 0.0), axis=1, keepdims=True)
        ts_in[it, d, 0] = jnp.where(lane == 64, top_energy, ts[:, 0:128])
        ts_in[it, d, 1] = ts[:, 128:256]
        spread(lambda p: ts_in.at[it, d], ts_in, it, ts_send, ts_recv, True)

        all_of(coarse, it, coarse_send, coarse_recv, True).wait_recv()
        group_next = group_now[...] - step_size * coarse[it].reshape(n_dev * ncon, nrhs)
        group_now[...] = group_next
        solved = dot3((ginv_hi[...], ginv_lo[...]), split(group_next))
        solved_own[it] = solved
        each_face(lambda b: solved_copy(it, b, opposite[b]).start())

        energy = inner_of_plain()
        own_coarse_now = group_now[pl.ds(pl.multiple_of(d * ncon, 16), ncon), :]
        dot_dev[it, d] = energy + fold(own_coarse_now * solved)
        spread(lambda p: dot_dev.at[it, d], dot_dev, it, dd_send, dd_recv, True)
        to_faces(prod, local_part)
        each_face(lambda b: face_copy(local_part, 2 * it + 1, b, opposite[b]).start())

        def advance(at, b, at_in, c):
            sol[at, :] = sol[at, :] + step_size * dirn[at, :]
            return c

        over_chunks(advance)

        @pl.when(it == ITERS)
        def _():
            pltpu.make_async_copy(sol, x_out, out_sem.at[0]).start()
            pltpu.make_async_copy(res, r_out, out_sem.at[1]).start()

        all_of(ts_in, it, ts_send, ts_recv, True).wait_recv()
        ts_all = jnp.concatenate(
            [ts_in[it, :, 0].reshape(nrhs, 128), ts_in[it, :, 1].reshape(nrhs, 128)], axis=1
        )
        upper[...] = dot3((tb_all_hi[...], tb_all_lo[...]), split(ts_all), NT)

        all_of(dot_dev, it, dd_send, dd_recv, True).wait_recv()
        line = lax.broadcasted_iota(jnp.int32, (8, nrhs), 0)
        dot_group[it, g] = jnp.sum(dot_dev[it], axis=0) + jnp.where(
            line == 0, upper[5 * ncon:5 * ncon + 1, :], 0.0
        )
        spread(lambda p: dot_group.at[it, g], dot_group, it, dg_send, dg_recv, False)

        own_hi, own_lo = split(solved + upper[0:ncon, :])
        each_face(lambda b: solved_copy(it, b, b).wait_recv())
        each_face(lambda b: face_copy(local_part, 2 * it + 1, b, b).wait_recv())

        def join(b, c):
            above = upper[pl.ds(pl.multiple_of((b + 1) * ncon, 16), ncon), :]
            in_hi, in_lo = split(solved_in[it, b] + above)
            values = jnp.concatenate(
                [own_hi, in_hi, own_lo, in_lo, jnp.zeros((256 - 4 * ncon, nrhs), BF16)], axis=0
            )
            at = pl.ds(pl.multiple_of(b * face, face), face)
            joined[at, :] = weight_of(b) * (
                local_part[at, :] + face_in[2 * it + 1, b] + dot(comb[at, :], values)
            )
            return c

        lax.fori_loop(0, 4, join, 0)
        from_faces(joined, prod)

        all_of(u_in, it, u_send, u_recv, True).wait_send()
        all_of(coarse, it, coarse_send, coarse_recv, True).wait_send()
        all_of(top_in, it, top_send, top_recv, False).wait_send()
        all_of(ts_in, it, ts_send, ts_recv, True).wait_send()
        all_of(dot_dev, it, dd_send, dd_recv, True).wait_send()

        def left(b):
            face_copy(field, 2 * it, b, opposite[b]).wait_send()
            face_copy(local_part, 2 * it + 1, b, opposite[b]).wait_send()
            parts_copy(it, b, opposite[b]).wait_send()
            solved_copy(it, b, opposite[b]).wait_send()

        each_face(left)

        @pl.when(later)
        def _():
            all_of(curv_dev, it, cd_send, cd_recv, True).wait_send()
            all_of(curv_group, it, cg_send, cg_recv, False).wait_send()
            all_of(dot_group, it, dg_send, dg_recv, False).wait_recv()
            norm_next = total(dot_group, it)
            step_now[...] = norm_next / norm_now[...]
            norm_now[...] = norm_next

        ratio = step_now[...]

        def turn(at, b, at_in, c):
            value = prod[at, :] + ratio * dirn[at, :]
            dirn[at, :] = value
            plain[at, :] = value.astype(BF16)
            return c

        over_chunks(turn)
        return carry

    lax.fori_loop(0, ITERS + 1, iteration, 0)

    store = pltpu.make_async_copy(dirn, d_out, out_sem.at[2])
    store.start()
    for m in range(ITERS + 1):
        all_of(dot_group, m, dg_send, dg_recv, False).wait_send()
    each_face(lambda b: basis_copy(b, opposite[b]).wait_send())
    each_face(lambda b: tb_copy(b, opposite[b]).wait_send())
    each_face(lambda b: tinv_copy(b, opposite[b]).wait_send(), (2, 3))
    pltpu.make_async_copy(sol, x_out, out_sem.at[0]).wait()
    pltpu.make_async_copy(res, r_out, out_sem.at[1]).wait()
    store.wait()


def local(
    n_group, n_dev,
    applied_loads, stiffness, local_inverse, coarse_basis, face_index, coarse_map, group_inverse, top_basis, top_inverse,
):
    ni, nrhs = applied_loads.shape[1:]
    ncon = coarse_basis.shape[1]
    topc = top_basis.shape[1]
    face = ni // 4
    per_dev = nrhs // n_dev
    uses = ITERS + 1
    exchanges = 2 * uses
    top_rows = n_group * 64
    top_pad = (n_group * topc + 127) // 128 * 128
    vmem = pl.BlockSpec(memory_space=pltpu.VMEM)
    smem = pl.BlockSpec(memory_space=pltpu.SMEM)
    hbm = pl.BlockSpec(memory_space=pl.ANY)
    field = jax.ShapeDtypeStruct((ni, nrhs), F32)
    dma = pltpu.SemaphoreType.DMA

    def f32(*shape):
        return pltpu.VMEM(shape, F32)

    def bf16(*shape):
        return pltpu.VMEM(shape, BF16)

    scratch = [
        f32(ni, nrhs), bf16(ni, ni), bf16(ni, ni), bf16(ncon, ni),
        pltpu.VMEM((ni // 128, 128), jnp.int32), pltpu.SMEM((1, ni), jnp.int32),
        f32(ni, nrhs),
        f32(ni, nrhs), f32(ni, nrhs), f32(ni, nrhs), f32(ni, nrhs), f32(ni, nrhs), f32(ni, nrhs), f32(ni, nrhs),
        bf16(ni, nrhs), bf16(ni, nrhs), bf16(ni, nrhs),
        f32(exchanges, 4, face, nrhs), f32(ncon, ni), f32(4, ncon, face), bf16(256, ni), f32(256, ni), bf16(ni, 256),
        bf16(ncon, n_dev * ncon), bf16(ncon, n_dev * ncon),
        f32(256, 256), bf16(256, 256), bf16(256, 256),
        bf16(top_rows, 256), bf16(top_rows, 256), f32(256, top_pad), f32(top_pad, 256),
        f32(ncon, 128), f32(4, ncon, 128), f32(topc, n_group * topc), f32(2, topc, n_group * topc), f32(256, nrhs),
        f32(uses, 256, nrhs), f32(uses, 4, ncon, nrhs), f32(uses, n_dev, ncon, nrhs),
        f32(uses, n_dev, 2, per_dev, 128), f32(uses, n_dev, 2, per_dev, 128),
        f32(uses, n_group, 2, per_dev, 128), f32(uses, n_dev, 2, per_dev, 128),
        f32(uses, ncon, nrhs), f32(uses, 4, ncon, nrhs),
        f32(n_dev * ncon, nrhs), f32(per_dev, n_group * 64), f32(1, nrhs), f32(nrhs, nrhs), f32(1, nrhs),
        f32(uses, n_dev, 8, nrhs), f32(uses, n_group, 8, nrhs),
        f32(uses, n_dev, 8, nrhs), f32(uses, n_group, 8, nrhs),
        dma((4 + ni // 128,)), dma((3,)), dma((exchanges, 4)), dma((exchanges, 4)),
        dma((4,)), dma((4,)), dma((4,)), dma((4,)), dma((2,)), dma((2,)),
        dma((uses, 4)), dma((uses, 4)), dma((uses, 4)), dma((uses, 4)),
    ] + [dma((uses,))] * 16
    x, r, dirn, one = pl.pallas_call(
        functools.partial(main_kernel, n_group, n_dev),
        out_shape=[field] * 3 + [jax.ShapeDtypeStruct((1, nrhs), F32)],
        in_specs=[hbm, hbm, hbm, hbm, smem, vmem, vmem, vmem, vmem],
        out_specs=[hbm] * 3 + [vmem],
        scratch_shapes=scratch,
        compiler_params=pltpu.CompilerParams(
            collective_id=0, has_side_effects=True, vmem_limit_bytes=56 * 2**20
        ),
        cost_estimate=pl.CostEstimate(
            flops=18 * ni * ni * nrhs, bytes_accessed=4 * ni * ni + 24 * ni * nrhs, transcendentals=0
        ),
        name="pcg",
    )(
        applied_loads[0], stiffness[0], local_inverse[0], coarse_basis[0],
        face_index, coarse_map, group_inverse, top_basis, top_inverse,
    )
    return (x * one)[None], (r * one)[None], (dirn * one)[None]


def solution(mesh):
    both = ("group", "dev")
    return jax.shard_map(
        functools.partial(local, mesh.shape["group"], mesh.shape["dev"]),
        mesh=mesh,
        in_specs=(
            P(both, None, None), P(both, None, None), P(both, None, None), P(both, None, None),
            P(both, None), P(both, None), P(both, None), P(both, None), P("group", None),
        ),
        out_specs=(P(both, None, None),) * 3,
        check_vma=False,
    )
```
